512 devices in a mesh: tm: 8 (over x, y_lo), mesh: 64 (over y_hi, z, core).
Axes of the slice: x: 4, y: 4 (y_hi: 2, y_lo: 2; y = y_hi * 2 + y_lo), z: 16, core: 2. Of those that a mesh axis runs over, the one named last changes fastest.
Arguments:
- iterate: float32 [3, 64, 512, 512], P(None, 'tm', 'mesh'), may hold values from -6 to 6
- forcing: float32 [3, 64, 512, 512], P(None, 'tm', 'mesh'), may hold values from -6 to 6
- start_state: float32 [3, 512, 512], P(None, 'mesh'), may hold values from -6 to 6
- damping: float32 [512, 512], P('mesh'), may hold values from 0.4 to 3
- coriolis: float32 [512, 512], P('mesh'), may hold values from -1 to 1
- coupling: float32 [512, 512], P('mesh'), may hold values from 0.04 to 0.12
- edge_order: int32 [64, 2, 512], P('mesh'), may hold values from 0 to 511, each once within a row
Outputs:
- updated: float32 [3, 64, 512, 512], P(None, 'tm', 'mesh')
The draws below stay inside these ranges and needn't reach their ends.
Inputs may be any that keep to these rules, and one draw needn't show every extreme that they name: edge_order[p,0] and edge_order[p,1] are each a permutation of 0..511.
All inputs are finite; a program needn't handle non-finite values.
Results may differ from the reference program's by a relative error of at most 0.0003.
Values sent between devices are 32-bit elements; how exact they have to be, the bound alone decides.
A program may use at most 64 MiB of HBM per device.

```python
import math
import jax
import jax.numpy as jnp
from jax import lax

STEPS = 8
ROWS = 8
COLS = 512
SWEEPS = 4
WINDOW = 64
PARTS_SIZE = 64
ALLROWS = 512
N_TM = 8


def block_levels(key, shape, cuts, low, top_value):
    def one(position, blocks):
        draws = jax.random.uniform(jax.random.fold_in(jax.random.fold_in(key, 6), position), (blocks,), jnp.float32, low / len(cuts), top_value / len(cuts))
        return jnp.repeat(jnp.exp(draws), shape[position] // blocks).reshape((-1,) + (1,) * (len(shape) - position - 1))

    level = one(*cuts[0])
    for cut in cuts[1:]:
        level = level * one(*cut)
    return level


def gaussian(rng, extent, deviation, reach, split=(), kind=jnp.bfloat16):
    entries = deviation * jax.random.normal(rng, extent, jnp.float32)
    if split:
        entries = entries * block_levels(rng, extent, split, -0.22, 0.18)
    return jnp.clip(entries, -reach, reach).astype(kind)


def setup_inputs(seed: int = 0) -> dict:
    arg_keys = jax.random.split(jax.random.key(seed), 8)
    return {
        "iterate": gaussian(arg_keys[0], (3, WINDOW, ALLROWS, COLS), 1.0, 6.0, ((1, 8), (2, 64)), jnp.float32),
        "forcing": gaussian(arg_keys[1], (3, WINDOW, ALLROWS, COLS), 1.0, 6.0, ((1, 8), (2, 64)), jnp.float32),
        "start_state": gaussian(arg_keys[2], (3, ALLROWS, COLS), 1.0, 6.0, ((1, 64),), jnp.float32),
        "damping": jnp.clip(jnp.exp(math.log(3.0) - 2.014903 * jax.random.uniform(arg_keys[3], (ALLROWS, COLS), jnp.float32) ** block_levels(arg_keys[3], (ALLROWS, COLS), ((0, 64),), -0.2, 0.2)), 0.4, 3.0),
        "coriolis": jnp.clip(jax.random.uniform(arg_keys[4], (ALLROWS, COLS), jnp.float32, -1.0, 1.0) * block_levels(arg_keys[4], (ALLROWS, COLS), ((0, 64),), -0.4, 0.0), -1.0, 1.0),
        "coupling": jnp.clip(jnp.exp(math.log(0.12) - 1.0986123 * jax.random.uniform(arg_keys[5], (ALLROWS, COLS), jnp.float32) ** block_levels(arg_keys[5], (ALLROWS, COLS), ((0, 64),), -0.2, 0.2)), 0.04, 0.12),
        "edge_order": jax.vmap(lambda own: jax.random.permutation(own, COLS))(jax.random.split(arg_keys[6], PARTS_SIZE * 2)).reshape((PARTS_SIZE, 2, COLS)).astype(jnp.int32),
    }


alpha_corner = 0.1
half_root = math.sqrt(3.0) / 2.0

def sample_rows(field):
    middle = field[..., 1:-1, :]
    upper = field[..., 2:, :]
    lower = field[..., :-2, :]
    east = jnp.roll(middle, -1, axis=-1)
    west = jnp.roll(middle, 1, axis=-1)
    north_west = jnp.roll(upper, 1, axis=-1)
    south_east = jnp.roll(lower, -1, axis=-1)
    along_x = east - west + 0.5 * (upper - north_west - lower + south_east)
    along_y = half_root * (upper + north_west - lower - south_east)
    return (along_x, along_y)

def couple(height, east_vel, north_vel, coupling):
    height_x, height_y = sample_rows(height)
    east_x, east_y = sample_rows(east_vel)
    north_x, north_y = sample_rows(north_vel)
    return (coupling * (east_x + north_y), coupling * height_x, coupling * height_y)

def phase_table(rows_idx, cols_idx, total):
    product = rows_idx[:, None] * cols_idx[None, :] % total
    angle = product.astype(jnp.float32) * (2.0 * math.pi / total)
    return (jnp.cos(angle), jnp.sin(angle))

def block_solve(source, lam_re, lam_im, damping, coriolis):
    a_re = lam_re + damping
    a_im = lam_im + 0.0 * damping
    a_abs = a_re * a_re + a_im * a_im
    h_re = (source[0, 0] * a_re + source[1, 0] * a_im) / a_abs
    h_im = (source[1, 0] * a_re - source[0, 0] * a_im) / a_abs
    d_re = a_re * a_re - a_im * a_im + coriolis * coriolis
    d_im = 2.0 * a_re * a_im
    d_abs = d_re * d_re + d_im * d_im
    nu_re = a_re * source[0, 1] - a_im * source[1, 1] + coriolis * source[0, 2]
    nu_im = a_re * source[1, 1] + a_im * source[0, 1] + coriolis * source[1, 2]
    nv_re = a_re * source[0, 2] - a_im * source[1, 2] - coriolis * source[0, 1]
    nv_im = a_re * source[1, 2] + a_im * source[0, 2] - coriolis * source[1, 1]
    u_re = (nu_re * d_re + nu_im * d_im) / d_abs
    u_im = (nu_im * d_re - nu_re * d_im) / d_abs
    v_re = (nv_re * d_re + nv_im * d_im) / d_abs
    v_im = (nv_im * d_re - nv_re * d_im) / d_abs
    return jnp.stack([jnp.stack([h_re, u_re, v_re]), jnp.stack([h_im, u_im, v_im])])

def pad_rows(field, edge_order):
    last = jnp.roll(field[..., -1, :], 1, axis=-2)
    first = jnp.roll(field[..., 0, :], -1, axis=-2)
    below = jnp.take_along_axis(last, jnp.broadcast_to(edge_order[:, 0, :], last.shape), axis=-1)
    above = jnp.take_along_axis(first, jnp.broadcast_to(edge_order[:, 1, :], first.shape), axis=-1)
    return jnp.concatenate([below[..., None, :], field, above[..., None, :]], axis=-2)

def reference(iterate, forcing, start_state, damping, coriolis, coupling, edge_order):
    total = STEPS * N_TM
    shape_five = (3, total, PARTS_SIZE, ROWS, COLS)
    field = iterate.reshape(shape_five)
    damp = damping.reshape(PARTS_SIZE, ROWS, COLS)
    rotate = coriolis.reshape(PARTS_SIZE, ROWS, COLS)
    weigh = coupling.reshape(PARTS_SIZE, ROWS, COLS)
    previous = jnp.concatenate([start_state[:, None], iterate[:, :-1]], axis=1).reshape(shape_five)
    padded = pad_rows(field, edge_order)
    off_h, off_u, off_v = couple(padded[0], padded[1], padded[2], weigh)
    applied = jnp.stack([damp * field[0] + off_h, damp * field[1] - rotate * field[2] + off_u, damp * field[2] + rotate * field[1] + off_v])
    residual = forcing.reshape(shape_five) + previous - field - applied
    log_alpha = math.log(alpha_corner)
    times = jnp.arange(total, dtype=jnp.int32)
    timef = times.astype(jnp.float32)
    scaled = residual * jnp.exp(timef * (log_alpha / total))[None, :, None, None, None]
    beta = math.exp(log_alpha / total)

    def one_freq(summed, freq):
        cos_t, sin_t = phase_table(freq[None], times, total)
        cos_r = cos_t[0]
        sin_r = sin_t[0]
        spec_re = jnp.einsum('n,cnpqw->cpqw', cos_r, scaled, precision=lax.Precision.HIGHEST)
        spec_im = -jnp.einsum('n,cnpqw->cpqw', sin_r, scaled, precision=lax.Precision.HIGHEST)
        spectrum = jnp.stack([spec_re, spec_im])
        angle = freq.astype(jnp.float32) * (2.0 * math.pi / total)
        lam_re = 1.0 - beta * jnp.cos(angle)
        lam_im = beta * jnp.sin(angle)
        solved = block_solve(spectrum, lam_re, lam_im, damp, rotate)
        for sweep in range(SWEEPS - 1):
            rims = pad_rows(solved, edge_order)
            off_h, off_u, off_v = couple(rims[:, 0], rims[:, 1], rims[:, 2], weigh)
            solved = block_solve(spectrum - jnp.stack([off_h, off_u, off_v], axis=1), lam_re, lam_im, damp, rotate)
        summed = summed + jnp.einsum('n,cpqw->cnpqw', cos_r, solved[0], precision=lax.Precision.HIGHEST) - jnp.einsum('n,cpqw->cnpqw', sin_r, solved[1], precision=lax.Precision.HIGHEST)
        return (summed, None)
    summed, _ = lax.scan(one_freq, jnp.zeros(shape_five, jnp.float32), times)
    unscale = jnp.exp(-timef * (log_alpha / total)) / total
    delta = summed * unscale[None, :, None, None, None]
    return (field + delta).reshape(3, total, ALLROWS, COLS)
```

```python
import functools
import math

import jax
import jax.numpy as jnp
import numpy as np
from jax import lax
from jax.experimental import pallas as pl
from jax.experimental.pallas import tpu as pltpu
from jax.sharding import PartitionSpec as P

MESH = pl.DeviceIdType.MESH
ALPHA = 0.1
HALF_ROOT = math.sqrt(3.0) / 2.0
SWEEPS = 4
G = 8
T = 64
L = 128
Q = 4
C = 3
WIDE = Q * C * L
LO, MID, HI = 0, 5, 15
EXT = 18


def tables():
    n = np.arange(T)
    forward = np.zeros((T, T))
    inverse = np.zeros((T, T))
    lam = np.zeros((2, T))
    beta = math.exp(math.log(ALPHA) / T)
    grow = ALPHA ** (n / T)
    for d in range(G):
        for half in range(2):
            for j in range(4):
                slot = 4 * d + j
                row = d * 8 + half * 4 + j
                if slot == 0:
                    freq, weight, part = 32 * half, 1.0, 0
                else:
                    freq, weight, part = slot, 2.0, half
                angle = 2.0 * math.pi * (freq * n % T) / T
                wave = np.cos(angle) if part == 0 else -np.sin(angle)
                forward[row] = wave * grow
                inverse[:, row] = weight * wave / grow / T
                lam[0, row] = 1.0 - beta * math.cos(2.0 * math.pi * freq / T)
                lam[1, row] = 0.0 if slot == 0 else beta * math.sin(2.0 * math.pi * freq / T)
    lam = np.broadcast_to(lam[:, :, None], (2, T, L))
    return [np.asarray(a, np.float32) for a in (forward, inverse, lam)]


def lanes(q, c):
    return pl.ds((q * C + c) * L, L)


def shift(tiles, step):
    lane = lax.broadcasted_iota(jnp.int32, (8, L), 1)
    turned = [pltpu.roll(t, step % L, axis=1) for t in tiles]
    edge = 0 if step == 1 else L - 1
    return [jnp.where(lane == edge, turned[(q - step) % Q], turned[q]) for q in range(Q)]


def permuted(tiles, order):
    out = []
    for q in range(Q):
        high = order[q] // L
        low = order[q] - high * L
        total = None
        for s in range(Q):
            part = jnp.take_along_axis(tiles[s], low, axis=1, mode="promise_in_bounds")
            total = part if total is None else jnp.where(high == s, part, total)
        out.append(total)
    return out


def couple(row, mid, low, up):
    s = HALF_ROOT
    h, u, v = range(3)
    diff = [[up[c][q] - low[c][q] for q in range(Q)] for c in range(3)]
    east = shift([mid[u][q] + 0.5 * low[u][q] - s * low[v][q] for q in range(Q)], -1)
    west = shift([mid[u][q] + 0.5 * up[u][q] - s * up[v][q] for q in range(Q)], 1)
    off_h = [east[q] - west[q] + 0.5 * diff[u][q] + s * diff[v][q] for q in range(Q)]
    low_m, up_p = shift(low[h], -1), shift(up[h], 1)
    mid_m, mid_p = shift(mid[h], -1), shift(mid[h], 1)
    off_u = [mid_m[q] - mid_p[q] + 0.5 * (diff[h][q] - up_p[q] + low_m[q]) for q in range(Q)]
    off_v = [s * (diff[h][q] + up_p[q] - low_m[q]) for q in range(Q)]
    return off_h, off_u, off_v


def load(ref, row):
    return [[ref[row, :, lanes(q, c)] for q in range(Q)] for c in range(C)]


def store(ref, row, tiles):
    for c in range(C):
        for q in range(Q):
            ref[row, :, lanes(q, c)] = tiles[c][q]


def wide(ref, q, i, row):
    return jnp.broadcast_to(ref[q, i, pl.ds(row, 1), :], (8, L))


def kernel(
    bands,
    it_any, fo_any, st_any, damp_any, cori_any, coup_any, order_any, fwd_ref, inv_ref, lam_ref,
    out_ref,
    it_v, fo_v, out_v, st_v, own_c, own_o, low_c, low_o, high_c, high_o, carry, fixed, first,
    rows_t, halo_lo, halo_hi, coef, spec, cur,
    a_send, a_recv, b_send, b_recv, c_send, c_recv, d_send, d_recv,
    in_sem, side_send, side_recv, a_ss, a_rs, b_ss, b_rs, c_ss, c_rs, d_ss, d_rs,
):
    me = lax.axis_index("tm")
    band = lax.axis_index("mesh")
    below = lax.rem(band + bands - 1, bands)
    above = lax.rem(band + 1, bands)

    def by_lanes(wide_ref, tiled_ref, sems, first, into):
        pairs = [(wide_ref.at[:, :, pl.ds(q * L, L)], tiled_ref.at[q]) for q in range(Q)]
        if not into:
            pairs = [(b, a) for a, b in pairs]
        return [pltpu.make_async_copy(a, b, sems.at[first + q]) for q, (a, b) in enumerate(pairs)]

    fields = by_lanes(it_any, it_v, in_sem, 7, True)
    forces = by_lanes(fo_any, fo_v, in_sem, 11, True)
    loads = [
        pltpu.make_async_copy(st_any, st_v, in_sem.at[2]),
        pltpu.make_async_copy(damp_any, fixed.at[0], in_sem.at[3]),
        pltpu.make_async_copy(cori_any, fixed.at[1], in_sem.at[4]),
        pltpu.make_async_copy(coup_any, fixed.at[2], in_sem.at[5]),
        pltpu.make_async_copy(order_any, own_o, in_sem.at[6]),
    ]
    for one in fields + loads + forces:
        one.start()
    barrier = pltpu.get_barrier_semaphore()
    for k in range(1, G):
        pl.semaphore_signal(barrier, 1, device_id={"tm": lax.rem(me + k, G)}, device_id_type=MESH)
    for p in (below, above):
        pl.semaphore_signal(barrier, 1, device_id={"mesh": p}, device_id_type=MESH)

    def side(index, src, dst, device):
        return pltpu.make_async_remote_copy(
            src_ref=src, dst_ref=dst, send_sem=side_send.at[index], recv_sem=side_recv.at[index],
            device_id=device, device_id_type=MESH,
        )

    def exchange(src, dst, ss, rs):
        return [
            pltpu.make_async_remote_copy(
                src_ref=src.at[lax.rem(me + k, G)], dst_ref=dst.at[me],
                send_sem=ss.at[k], recv_sem=rs.at[k],
                device_id={"tm": lax.rem(me + k, G)}, device_id_type=MESH,
            )
            for k in range(1, G)
        ]

    for one in fields:
        one.wait()
    for r in range(8):
        for c in range(C):
            for q in range(Q):
                rows_t[r + 1, :, lanes(q, c)] = it_v[q, c, pl.ds(r, 8, stride=8), :]
    for one in loads:
        one.wait()
    for q in range(Q):
        for i in range(3):
            own_c[q, i] = fixed[i, :, pl.ds(q * L, L)]
    pl.semaphore_wait(barrier, G + 1)
    to_next = {"tm": lax.rem(me + 1, G)}
    sides = [
        side(0, rows_t.at[1], halo_hi, {"mesh": below}),
        side(1, rows_t.at[8], halo_lo, {"mesh": above}),
        side(2, it_v.at[:, :, pl.ds(56, 8), :], carry, to_next),
        side(3, own_c, high_c, {"mesh": below}),
        side(4, own_c, low_c, {"mesh": above}),
        side(5, own_o, high_o, {"mesh": below}),
        side(6, own_o, low_o, {"mesh": above}),
    ]
    for one in sides:
        one.start()

    def order(ref, which):
        return [jnp.broadcast_to(ref[pl.ds(which, 1), pl.ds(q * L, L)], (8, L)) for q in range(Q)]

    for one in forces:
        one.wait()
    for index in (0, 1, 2):
        sides[index].wait_recv()
    low = [[halo_lo[:, lanes(q, c)] for q in range(Q)] for c in range(C)]
    store(rows_t, 0, [permuted(low[c], order(own_o, 0)) for c in range(C)])
    high = [[halo_hi[:, lanes(q, c)] for q in range(Q)] for c in range(C)]
    store(rows_t, 9, [permuted(high[c], order(own_o, 1)) for c in range(C)])

    for q in range(Q):
        for c in range(C):
            first[q, c] = jnp.where(me == 0, st_v[c, :, pl.ds(q * L, L)], carry[q, c])
    sub = lax.broadcasted_iota(jnp.int32, (8, L), 0)

    def residual_row(r, _):
        mid = load(rows_t, r + 1)
        off = couple(r, mid, load(rows_t, r), load(rows_t, r + 2))
        for q in range(Q):
            damp, cori, coup = [wide(own_c, q, i, r) for i in range(3)]
            h, u, v = mid[0][q], mid[1][q], mid[2][q]
            applied = [damp * h, damp * u - cori * v, damp * v + cori * u]
            target = lax.rem(r - 2 * q + 16, G)
            for c in range(C):
                before = jnp.where(sub == 0, wide(first, q, c, r), pltpu.roll(mid[c][q], 1, axis=0))
                force = fo_v[q, c, pl.ds(r, 8, stride=8), :]
                a_send[target, :, lanes(q, c)] = (
                    force + before - mid[c][q] - (applied[c] + coup * off[c][q])
                )
        return 0

    lax.fori_loop(0, 8, residual_row, 0)
    hop_a = exchange(a_send, a_recv, a_ss, a_rs)
    for one in hop_a:
        one.start()
    a_recv[me] = a_send[me]

    for index in (3, 4, 5, 6):
        sides[index].wait_recv()
    lam_re = lam_ref[0, pl.ds(me * 8, 8), :]
    lam_im = lam_ref[1, pl.ds(me * 8, 8), :]
    sign = jnp.where(sub < 4, -1.0, 1.0)

    def coef_row(ref, offset):
        def body(r, _):
            for q in range(Q):
                damp, cori, coup = [wide(ref, q, i, r) for i in range(3)]
                a_re = lam_re + damp
                a_im = lam_im
                inv = 1.0 / (a_re * a_re + a_im * a_im)
                d_re = a_re * a_re - a_im * a_im + cori * cori
                d_im = 2.0 * a_re * a_im
                d_inv = 1.0 / (d_re * d_re + d_im * d_im)
                six = [
                    a_re * inv,
                    -sign * a_im * inv,
                    (a_re * d_re + a_im * d_im) * d_inv,
                    sign * (a_im * d_re - a_re * d_im) * d_inv,
                    cori * d_re * d_inv,
                    -sign * cori * d_im * d_inv,
                    coup,
                ]
                for i in range(7):
                    coef[r + offset, i, :, pl.ds(q * L, L)] = six[i]
            return 0

        return body

    for ref, start, stop, offset in ((own_c, 0, 8, MID), (low_c, 5, 8, LO - 5), (high_c, 0, 3, HI)):
        lax.fori_loop(start, stop, coef_row(ref, offset), 0)

    for one in hop_a:
        one.wait_recv()
    high_prec = lax.Precision.HIGHEST
    b_send[...] = jnp.dot(
        fwd_ref[...], a_recv[...].reshape(T, WIDE), precision=high_prec, preferred_element_type=jnp.float32
    ).reshape(G, 8, WIDE)
    hop_b = exchange(b_send, b_recv, b_ss, b_rs)
    for one in hop_b:
        one.start()
    b_recv[me] = b_send[me]
    for one in hop_b:
        one.wait_recv()
    for r in range(8):
        for q in range(Q):
            for c in range(C):
                spec[MID + r, :, lanes(q, c)] = b_recv[(r - 2 * q) % G, :, lanes(q, c)]
    rims = [
        side(7, spec.at[pl.ds(MID, 3)], spec.at[pl.ds(HI, 3)], {"mesh": below}),
        side(8, spec.at[pl.ds(MID + 5, 3)], spec.at[pl.ds(LO, 3)], {"mesh": above}),
    ]
    for one in rims:
        one.start()

    def solve(row, x):
        out = [[], [], []]
        for q in range(Q):
            k = [coef[row, i, :, pl.ds(q * L, L)] for i in range(6)]
            xh, xu, xv = x[0][q], x[1][q], x[2][q]
            sh, su, sv = [pltpu.roll(t, 4, axis=0) for t in (xh, xu, xv)]
            out[0].append(k[0] * xh + k[1] * sh)
            out[1].append(k[2] * xu + k[3] * su + (k[4] * xv + k[5] * sv))
            out[2].append(k[2] * xv + k[3] * sv - (k[4] * xu + k[5] * su))
        return out

    def first_row(row, _):
        store(cur.at[0], row, solve(row, load(spec, row)))
        return 0

    def sweep_row(src, dst):
        def body(row, _):
            off = couple(row, load(src, row), load(src, row - 1), load(src, row + 1))
            full = load(spec, row)
            x = [
                [full[c][q] - coef[row, 6, :, pl.ds(q * L, L)] * off[c][q] for q in range(Q)]
                for c in range(C)
            ]
            store(dst, row, solve(row, x))
            return 0

        return body

    lax.fori_loop(MID, MID + 8, first_row, 0)
    for one in rims:
        one.wait_recv()
    lax.fori_loop(LO, LO + 3, first_row, 0)
    lax.fori_loop(HI, HI + 3, first_row, 0)
    for sweep in range(SWEEPS - 1):
        src, dst = cur.at[sweep % 2], cur.at[(sweep + 1) % 2]
        reach = SWEEPS - 2 - sweep
        ghosts = [(MID - 1, LO + 2, own_o, 0), (MID + 8, HI, own_o, 1)]
        if reach:
            ghosts += [(LO + 3, MID, low_o, 1), (HI - 1, MID + 7, high_o, 0)]
        for to, source, ref, which in ghosts:
            tiles = load(src, source)
            store(src, to, [permuted(tiles[c], order(ref, which)) for c in range(C)])
        body = sweep_row(src, dst)
        if reach:
            lax.fori_loop(LO + 3 - reach, LO + 3, body, 0)
        lax.fori_loop(MID, MID + 8, body, 0)
        if reach:
            lax.fori_loop(HI, HI + reach, body, 0)

    last = cur.at[(SWEEPS - 1) % 2]
    for r in range(8):
        for q in range(Q):
            for c in range(C):
                c_send[(r - 2 * q) % G, :, lanes(q, c)] = last[MID + r, :, lanes(q, c)]
    hop_c = exchange(c_send, c_recv, c_ss, c_rs)
    for one in hop_c:
        one.start()
    c_recv[me] = c_send[me]
    for one in hop_c:
        one.wait_recv()
    d_send[...] = jnp.dot(
        inv_ref[...], c_recv[...].reshape(T, WIDE), precision=high_prec, preferred_element_type=jnp.float32
    ).reshape(G, 8, WIDE)
    hop_d = exchange(d_send, d_recv, d_ss, d_rs)
    for one in hop_d:
        one.start()
    d_recv[me] = d_send[me]
    for one in hop_d:
        one.wait_recv()
    for r in range(8):
        for q in range(Q):
            for c in range(C):
                out_v[q, c, pl.ds(r, 8, stride=8), :] = (
                    rows_t[r + 1, :, lanes(q, c)] + d_recv[(r - 2 * q) % G, :, lanes(q, c)]
                )
    outs = by_lanes(out_ref, out_v, in_sem, 7, False)
    for one in outs:
        one.start()
    for one in outs:
        one.wait()
    for one in sides + rims + hop_a + hop_b + hop_c + hop_d:
        one.wait_send()


def on_device(bands, iterate, forcing, start_state, damping, coriolis, coupling, edge_order):
    forward, inverse, lam = tables()
    flat = (C, T, Q * L)
    hbm, vmem = pl.BlockSpec(memory_space=pl.ANY), pl.BlockSpec(memory_space=pltpu.VMEM)
    f32, i32 = jnp.float32, jnp.int32
    block = pltpu.VMEM((G, 8, WIDE), f32)
    staged = pltpu.VMEM((3, 8, Q * L), f32)
    own, pair = pltpu.VMEM((Q, 3, 8, L), f32), pltpu.VMEM((2, Q * L), i32)
    tiled = pltpu.VMEM((Q, C, T, L), f32)
    row = pltpu.VMEM((8, WIDE), f32)
    hops = pltpu.SemaphoreType.DMA((G,))
    out = pl.pallas_call(
        functools.partial(kernel, bands),
        out_shape=jax.ShapeDtypeStruct(flat, f32),
        in_specs=[hbm] * 7 + [vmem] * 3,
        out_specs=hbm,
        scratch_shapes=[
            tiled, tiled, tiled, staged, own, pair, own, pair, own, pair, own, staged, own,
            pltpu.VMEM((10, 8, WIDE), f32), row, row,
            pltpu.VMEM((EXT, 7, 8, Q * L), f32),
            pltpu.VMEM((EXT, 8, WIDE), f32),
            pltpu.VMEM((2, EXT, 8, WIDE), f32),
        ]
        + [block] * 8
        + [pltpu.SemaphoreType.DMA((15,)), pltpu.SemaphoreType.DMA((9,)), pltpu.SemaphoreType.DMA((9,))]
        + [hops] * 8,
        compiler_params=pltpu.CompilerParams(
            collective_id=0, has_side_effects=True, vmem_limit_bytes=32 * 1024 * 1024
        ),
    )(
        iterate.reshape(flat), forcing.reshape(flat), start_state, damping, coriolis, coupling,
        edge_order.reshape(2, Q * L), forward, inverse, lam,
    )
    return out.reshape(iterate.shape)


def solution(mesh):
    in_specs = (
        P(None, "tm", "mesh", None),
        P(None, "tm", "mesh", None),
        P(None, "mesh", None),
        P("mesh", None),
        P("mesh", None),
        P("mesh", None),
        P("mesh", None, None),
    )
    return jax.shard_map(
        functools.partial(on_device, mesh.shape["mesh"]),
        mesh=mesh, in_specs=in_specs, out_specs=P(None, "tm", "mesh", None), check_vma=False,
    )
```

```python
import functools
import math

import jax
import jax.numpy as jnp
import numpy as np
from jax import lax
from jax.experimental import pallas as pl
from jax.experimental.pallas import tpu as pltpu
from jax.sharding import PartitionSpec as P

MESH = pl.DeviceIdType.MESH
ALPHA = 0.1
HALF_ROOT = math.sqrt(3.0) / 2.0
SWEEPS = 4
G = 8
T = 64
L = 128
Q = 4
C = 3
WIDE = Q * C * L
BLOCK = C * L
LO, MID, HI = 0, 5, 15
EXT = 18
FORTH = ((0, 3), (3, 1))
BACK = ((0, 1), (1, 2), (3, 1))
FAR = ((2, 1), (2, 0), (1, 1), (3, 1), (1, 0), (3, 0), (0, 1))


def tables():
    n = np.arange(T)
    forward = np.zeros((T, T))
    inverse = np.zeros((T, T))
    lam = np.zeros((2, T))
    beta = math.exp(math.log(ALPHA) / T)
    grow = ALPHA ** (n / T)
    for d in range(G):
        for half in range(2):
            for j in range(4):
                slot = 4 * d + j
                row = d * 8 + half * 4 + j
                if slot == 0:
                    freq, weight, part = 32 * half, 1.0, 0
                else:
                    freq, weight, part = slot, 2.0, half
                angle = 2.0 * math.pi * (freq * n % T) / T
                wave = np.cos(angle) if part == 0 else -np.sin(angle)
                forward[row] = wave * grow
                inverse[:, row] = weight * wave / grow / T
                lam[0, row] = 1.0 - beta * math.cos(2.0 * math.pi * freq / T)
                lam[1, row] = 0.0 if slot == 0 else beta * math.sin(2.0 * math.pi * freq / T)
    later = np.concatenate([forward[:, 8::8], np.zeros((T, 1))], axis=1)
    forward = np.concatenate([forward, later], axis=1)
    lam = np.broadcast_to(lam[:, :, None], (2, T, L))
    return [np.asarray(a, np.float32) for a in (forward, inverse, lam)]


def lanes(q, c):
    return pl.ds((q * C + c) * L, L)


def shift(tiles, step):
    lane = lax.broadcasted_iota(jnp.int32, (8, L), 1)
    turned = [pltpu.roll(t, step % L, axis=1) for t in tiles]
    edge = 0 if step == 1 else L - 1
    return [jnp.where(lane == edge, turned[(q - step) % Q], turned[q]) for q in range(Q)]


def permuted(tiles, order):
    out = []
    for q in range(Q):
        high = order[q] // L
        low = order[q] - high * L
        total = None
        for s in range(Q):
            part = jnp.take_along_axis(tiles[s], low, axis=1, mode="promise_in_bounds")
            total = part if total is None else jnp.where(high == s, part, total)
        out.append(total)
    return out


def couple(row, mid, low, up):
    s = HALF_ROOT
    h, u, v = range(3)
    diff = [[up[c][q] - low[c][q] for q in range(Q)] for c in range(3)]
    east = shift([mid[u][q] + 0.5 * low[u][q] - s * low[v][q] for q in range(Q)], -1)
    west = shift([mid[u][q] + 0.5 * up[u][q] - s * up[v][q] for q in range(Q)], 1)
    off_h = [east[q] - west[q] + 0.5 * diff[u][q] + s * diff[v][q] for q in range(Q)]
    low_m, up_p = shift(low[h], -1), shift(up[h], 1)
    mid_m, mid_p = shift(mid[h], -1), shift(mid[h], 1)
    off_u = [mid_m[q] - mid_p[q] + 0.5 * (diff[h][q] - up_p[q] + low_m[q]) for q in range(Q)]
    off_v = [s * (diff[h][q] + up_p[q] - low_m[q]) for q in range(Q)]
    return off_h, off_u, off_v


def load(ref, row):
    return [[ref[row, :, lanes(q, c)] for q in range(Q)] for c in range(C)]


def store(ref, row, tiles):
    for c in range(C):
        for q in range(Q):
            ref[row, :, lanes(q, c)] = tiles[c][q]


def wide(ref, q, i, row):
    return jnp.broadcast_to(ref[q, i, pl.ds(row, 1), :], (8, L))


def kernel(
    bands,
    it_any, fo_any, st_any, damp_any, cori_any, coup_any, order_any, fwd_any, inv_any, lam_any,
    out_ref,
    fwd_ref, inv_ref, lam_ref, it_v, fo_v, out_v, st_v, fixed,
    own_c, own_o, low_c, low_o, high_c, high_o, first,
    rows_t, halo_lo, halo_hi, coef, spec, cur,
    e_recv, a_send, a_recv, b_send, b_recv, c_send, c_recv, d_send, d_recv,
    in_sem, side_send, side_recv, e_ss, e_rs, a_ss, a_rs, b_ss, b_rs, c_ss, c_rs, d_ss, d_rs,
):
    me = lax.axis_index("tm")
    me_x, me_y = me // 2, lax.rem(me, 2)
    band = lax.axis_index("mesh")
    below = lax.rem(band + bands - 1, bands)
    above = lax.rem(band + 1, bands)
    peers = [lax.rem(me_x + dx, 4) * 2 + lax.rem(me_y + dy, 2) for dx, dy in FAR]

    def by_lanes(wide_ref, tiled_ref, base, into):
        pairs = [(wide_ref.at[:, :, pl.ds(q * L, L)], tiled_ref.at[q]) for q in range(Q)]
        if not into:
            pairs = [(b, a) for a, b in pairs]
        return [pltpu.make_async_copy(a, b, in_sem.at[base + q]) for q, (a, b) in enumerate(pairs)]

    fields = by_lanes(it_any, it_v, 0, True)
    forces = by_lanes(fo_any, fo_v, 4, True)
    loads = [
        pltpu.make_async_copy(source, target, in_sem.at[8 + i])
        for i, (source, target) in enumerate(
            [
                (st_any, st_v), (damp_any, fixed.at[0]), (cori_any, fixed.at[1]), (coup_any, fixed.at[2]),
                (order_any, own_o), (fwd_any, fwd_ref), (inv_any, inv_ref), (lam_any, lam_ref),
            ]
        )
    ]
    for one in fields + forces + loads:
        one.start()
    barrier = pltpu.get_barrier_semaphore()
    for peer in peers:
        pl.semaphore_signal(barrier, 1, device_id={"tm": peer}, device_id_type=MESH)
    for p in (below, above):
        pl.semaphore_signal(barrier, 1, device_id={"mesh": p}, device_id_type=MESH)

    sent = []

    def remote(src, dst, ss, rs, device):
        one = pltpu.make_async_remote_copy(
            src_ref=src, dst_ref=dst, send_sem=ss, recv_sem=rs, device_id=device, device_id_type=MESH
        )
        sent.append(one)
        return one

    def side(index, src, dst, p):
        return remote(src, dst, side_send.at[index], side_recv.at[index], {"mesh": p})

    def hop(src, dst, ss, rs, groups, index):
        start, count = groups[index]
        part = pl.ds(start, count)
        return [
            remote(
                src.at[peer, part], dst.at[me, part],
                ss.at[index * 7 + k], rs.at[index * 7 + k], {"tm": peer},
            )
            for k, peer in enumerate(peers)
        ]

    def start(copies):
        for one in copies:
            one.start()

    def arrive(copies):
        for one in copies:
            one.wait_recv()

    def keep(src, dst, group):
        for m in range(group[0], group[0] + group[1]):
            dst[me, m] = src[me, m]

    for one in fields:
        one.wait()
    for r in range(8):
        for c in range(C):
            for q in range(Q):
                rows_t[r + 1, :, lanes(q, c)] = it_v[q, c, pl.ds(r, 8, stride=8), :]
    for one in loads + forces:
        one.wait()
    for q in range(Q):
        for i in range(3):
            own_c[q, i] = fixed[i, :, pl.ds(q * L, L)]
            first[q, i] = jnp.where(me == 0, st_v[i, :, pl.ds(q * L, L)], 0.0)

    sub = lax.broadcasted_iota(jnp.int32, (8, L), 0)

    def residual_row(r, half, m):
        mid = load(rows_t, r + 1)
        off = couple(r, mid, load(rows_t, r), load(rows_t, r + 2))
        for q in range(Q):
            damp, cori, coup = [wide(own_c, q, i, r) for i in range(3)]
            h, u, v = mid[0][q], mid[1][q], mid[2][q]
            applied = [damp * h, damp * u - cori * v, damp * v + cori * u]
            for c in range(C):
                before = jnp.where(sub == 0, wide(first, q, c, r), pltpu.roll(mid[c][q], 1, axis=0))
                force = fo_v[q, c, pl.ds(r, 8, stride=8), :]
                a_send[2 * q + half, m, :, pl.ds(c * L, L)] = (
                    force + before - mid[c][q] - (applied[c] + coup * off[c][q])
                )

    def residual_pair(m, _):
        residual_row(3 - m, 0, m)
        residual_row(4 + m, 1, m)
        return 0

    lax.fori_loop(0, 3, residual_pair, 0)

    pl.semaphore_wait(barrier, 9)
    halos = [side(0, rows_t.at[1], halo_hi, below), side(1, rows_t.at[8], halo_lo, above)]
    start(halos)
    last = pl.ds(T - 8, 8)
    hop_e = [
        remote(it_v.at[peer // 2, :, last, :], e_recv.at[me], e_ss.at[k], e_rs.at[k], {"tm": peer})
        for k, peer in enumerate(peers)
    ]
    start(hop_e)
    hop_a = [hop(a_send, a_recv, a_ss, a_rs, FORTH, i) for i in range(len(FORTH))]
    start(hop_a[0])
    params = [
        side(2, own_c, high_c, below), side(3, own_c, low_c, above),
        side(4, own_o, high_o, below), side(5, own_o, low_o, above),
    ]
    start(params)
    e_recv[me] = it_v[me_x, :, last, :]
    keep(a_send, a_recv, FORTH[0])

    def order(ref, which):
        return [jnp.broadcast_to(ref[pl.ds(which, 1), pl.ds(q * L, L)], (8, L)) for q in range(Q)]

    def halo(ref, row, which):
        tiles = [[ref[:, lanes(q, c)] for q in range(Q)] for c in range(C)]
        store(rows_t, row, [permuted(tiles[c], order(own_o, which)) for c in range(C)])

    arrive(halos)
    halo(halo_lo, 0, 0)
    halo(halo_hi, 9, 1)
    residual_pair(3, 0)
    start(hop_a[1])
    keep(a_send, a_recv, FORTH[1])

    lam_re = lam_ref[0, pl.ds(me * 8, 8), :]
    lam_im = lam_ref[1, pl.ds(me * 8, 8), :]
    sign = jnp.where(sub < 4, -1.0, 1.0)

    def coef_row(ref, offset):
        def body(r, _):
            for q in range(Q):
                damp, cori, coup = [wide(ref, q, i, r) for i in range(3)]
                a_re = lam_re + damp
                a_im = lam_im
                inv = 1.0 / (a_re * a_re + a_im * a_im)
                d_re = a_re * a_re - a_im * a_im + cori * cori
                d_im = 2.0 * a_re * a_im
                d_inv = 1.0 / (d_re * d_re + d_im * d_im)
                seven = [
                    a_re * inv,
                    -sign * a_im * inv,
                    (a_re * d_re + a_im * d_im) * d_inv,
                    sign * (a_im * d_re - a_re * d_im) * d_inv,
                    cori * d_re * d_inv,
                    -sign * cori * d_im * d_inv,
                    coup,
                ]
                for i in range(7):
                    coef[r + offset, i, :, pl.ds(q * L, L)] = seven[i]
            return 0

        return body

    lax.fori_loop(0, 8, coef_row(own_c, MID), 0)

    def transform(table, src, dst, m, extra):
        rows = src[:, m].reshape(T, BLOCK)
        if extra is not None:
            rows = jnp.concatenate([rows, extra], axis=0)
        dst[:, m] = jnp.dot(
            table, rows, precision=lax.Precision.HIGHEST, preferred_element_type=jnp.float32
        ).reshape(G, 8, BLOCK)

    def previous(m):
        row = 3 - m + me_y * (1 + 2 * m)
        return jnp.concatenate([e_flat(c, row) for c in range(C)], axis=1)

    def e_flat(c, row):
        return e_recv.reshape(G * C * 8, L)[pl.ds(c * 8 + row, G, stride=C * 8), :]

    arrive(hop_e)
    hop_b = [hop(b_send, b_recv, b_ss, b_rs, FORTH, i) for i in range(len(FORTH))]
    for i, (begin, count) in enumerate(FORTH):
        arrive(hop_a[i])
        for m in range(begin, begin + count):
            transform(fwd_ref[...], a_recv, b_send, m, previous(m))
        start(hop_b[i])
        keep(b_send, b_recv, FORTH[i])

    arrive(params)
    lax.fori_loop(5, 8, coef_row(low_c, LO - 5), 0)
    lax.fori_loop(0, 3, coef_row(high_c, HI), 0)

    def solve(row, x):
        out = [[], [], []]
        for q in range(Q):
            k = [coef[row, i, :, pl.ds(q * L, L)] for i in range(6)]
            xh, xu, xv = x[0][q], x[1][q], x[2][q]
            sh, su, sv = [pltpu.roll(t, 4, axis=0) for t in (xh, xu, xv)]
            out[0].append(k[0] * xh + k[1] * sh)
            out[1].append(k[2] * xu + k[3] * su + (k[4] * xv + k[5] * sv))
            out[2].append(k[2] * xv + k[3] * sv - (k[4] * xu + k[5] * su))
        return out

    def first_row(row):
        store(cur.at[0], row, solve(row, load(spec, row)))

    def sweep_row(level, row):
        src = cur.at[level]
        off = couple(row, load(src, row), load(src, row - 1), load(src, row + 1))
        full = load(spec, row)
        x = [
            [full[c][q] - coef[row, 6, :, pl.ds(q * L, L)] * off[c][q] for q in range(Q)]
            for c in range(C)
        ]
        return solve(row, x)

    def sweep_pair(level, low, high):
        def body(i, _):
            store(cur.at[level + 1], low + i, sweep_row(level, low + i))
            store(cur.at[level + 1], high - i, sweep_row(level, high - i))
            return 0

        return body

    def ghost(level, to, source, ref, which):
        src = cur.at[level]
        tiles = load(src, source)
        store(src, to, [permuted(tiles[c], order(ref, which)) for c in range(C)])

    def own_rows(m, _):
        for half, r in ((0, 3 - m), (1, 4 + m)):
            for q in range(Q):
                for c in range(C):
                    spec[MID + r, :, lanes(q, c)] = b_recv[2 * q + half, m, :, pl.ds(c * L, L)]
        return 0

    def own_first(m, _):
        first_row(MID + 3 - m)
        first_row(MID + 4 + m)
        return 0

    def rim(index, src, dst, count, p):
        return side(index, spec.at[pl.ds(src, count)], spec.at[pl.ds(dst, count)], p)

    rims = [
        rim(6, MID + 1, HI + 1, 2, below), rim(7, MID + 5, LO, 2, above),
        rim(8, MID, HI, 1, below), rim(9, MID + 7, LO + 2, 1, above),
    ]
    arrive(hop_b[0])
    lax.fori_loop(0, 3, own_rows, 0)
    start(rims[:2])
    lax.fori_loop(0, 3, own_first, 0)
    lax.fori_loop(0, 2, sweep_pair(0, MID + 2, MID + 5), 0)
    arrive(hop_b[1])
    own_rows(3, 0)
    start(rims[2:])
    own_first(3, 0)
    ghost(0, LO + 3, MID, low_o, 1)
    ghost(0, HI - 1, MID + 7, high_o, 0)
    lax.fori_loop(0, 1, sweep_pair(0, MID + 1, MID + 6), 0)
    lax.fori_loop(0, 2, sweep_pair(1, MID + 2, MID + 5), 0)

    hop_c = [hop(c_send, c_recv, c_ss, c_rs, BACK, i) for i in range(len(BACK))]

    def last_pair(m):
        for half, r in ((0, 3 - m), (1, 4 + m)):
            tiles = sweep_row(2, MID + r)
            for q in range(Q):
                for c in range(C):
                    c_send[2 * q + half, m, :, pl.ds(c * L, L)] = tiles[c][q]

    def finish(i):
        begin, count = BACK[i]
        if count == 1:
            last_pair(begin)
        else:
            def body(m, _):
                last_pair(m)
                return 0

            lax.fori_loop(begin, begin + count, body, 0)
        start(hop_c[i])
        keep(c_send, c_recv, BACK[i])

    finish(0)
    arrive(rims)

    def rim_first(i, _):
        first_row(LO + i)
        first_row(HI + 2 - i)
        return 0

    lax.fori_loop(0, 3, rim_first, 0)
    ghost(0, MID - 1, LO + 2, own_o, 0)
    ghost(0, MID + 8, HI, own_o, 1)
    lax.fori_loop(0, 2, sweep_pair(0, LO + 1, HI + 1), 0)
    lax.fori_loop(0, 1, sweep_pair(0, MID, MID + 7), 0)
    ghost(1, LO + 3, MID, low_o, 1)
    ghost(1, HI - 1, MID + 7, high_o, 0)
    ghost(1, MID - 1, LO + 2, own_o, 0)
    ghost(1, MID + 8, HI, own_o, 1)
    lax.fori_loop(0, 1, sweep_pair(1, LO + 2, HI), 0)
    lax.fori_loop(0, 2, sweep_pair(1, MID, MID + 7), 0)
    ghost(2, MID - 1, LO + 2, own_o, 0)
    ghost(2, MID + 8, HI, own_o, 1)
    for i in range(1, len(BACK)):
        finish(i)

    hop_d = [hop(d_send, d_recv, d_ss, d_rs, BACK, i) for i in range(len(BACK))]
    for i, (begin, count) in enumerate(BACK):
        arrive(hop_c[i])
        for m in range(begin, begin + count):
            transform(inv_ref[...], c_recv, d_send, m, None)
        start(hop_d[i])
        keep(d_send, d_recv, BACK[i])
    for i, (begin, count) in enumerate(BACK):
        arrive(hop_d[i])
        for m in range(begin, begin + count):
            for half, r in ((0, 3 - m), (1, 4 + m)):
                for q in range(Q):
                    for c in range(C):
                        out_v[q, c, pl.ds(r, 8, stride=8), :] = (
                            rows_t[r + 1, :, lanes(q, c)] + d_recv[2 * q + half, m, :, pl.ds(c * L, L)]
                        )
    outs = by_lanes(out_ref, out_v, 0, False)
    for one in outs:
        one.start()
    for one in outs:
        one.wait()
    for one in sent:
        one.wait_send()


def on_device(bands, iterate, forcing, start_state, damping, coriolis, coupling, edge_order):
    forward, inverse, lam = tables()
    flat = (C, T, Q * L)
    hbm = pl.BlockSpec(memory_space=pltpu.HBM)
    f32, i32 = jnp.float32, jnp.int32
    block = pltpu.VMEM((G, 4, 8, BLOCK), f32)
    staged = pltpu.VMEM((3, 8, Q * L), f32)
    own, pair = pltpu.VMEM((Q, 3, 8, L), f32), pltpu.VMEM((2, Q * L), i32)
    tiled = pltpu.VMEM((Q, C, T, L), f32)
    row = pltpu.VMEM((8, WIDE), f32)
    dma = pltpu.SemaphoreType.DMA
    out = pl.pallas_call(
        functools.partial(kernel, bands),
        out_shape=jax.ShapeDtypeStruct(flat, f32),
        in_specs=[hbm] * 10,
        out_specs=hbm,
        scratch_shapes=[
            pltpu.VMEM((T, T + 8), f32), pltpu.VMEM((T, T), f32), pltpu.VMEM((2, T, L), f32),
            tiled, tiled, tiled, staged, staged,
            own, pair, own, pair, own, pair, own,
            pltpu.VMEM((10, 8, WIDE), f32), row, row,
            pltpu.VMEM((EXT, 7, 8, Q * L), f32),
            pltpu.VMEM((EXT, 8, WIDE), f32),
            pltpu.VMEM((SWEEPS, EXT, 8, WIDE), f32),
            pltpu.VMEM((G, C, 8, L), f32),
        ]
        + [block] * 8
        + [dma((16,)), dma((10,)), dma((10,)), dma((7,)), dma((7,))]
        + [dma((7 * len(FORTH),))] * 4
        + [dma((7 * len(BACK),))] * 4,
        compiler_params=pltpu.CompilerParams(
            collective_id=0, has_side_effects=True, vmem_limit_bytes=60 * 1024 * 1024
        ),
    )(
        iterate.reshape(flat), forcing.reshape(flat), start_state, damping, coriolis, coupling,
        edge_order.reshape(2, Q * L), forward, inverse, lam,
    )
    return out.reshape(iterate.shape)


def solution(mesh):
    in_specs = (
        P(None, "tm", "mesh", None),
        P(None, "tm", "mesh", None),
        P(None, "mesh", None),
        P("mesh", None),
        P("mesh", None),
        P("mesh", None),
        P("mesh", None, None),
    )
    return jax.shard_map(
        functools.partial(on_device, mesh.shape["mesh"]),
        mesh=mesh, in_specs=in_specs, out_specs=P(None, "tm", "mesh", None), check_vma=False,
    )
```

```python
import functools
import math

import jax
import jax.numpy as jnp
import numpy as np
from jax import lax
from jax.experimental import pallas as pl
from jax.experimental.pallas import tpu as pltpu
from jax.sharding import PartitionSpec as P

MESH = pl.DeviceIdType.MESH
ALPHA = 0.1
HALF_ROOT = math.sqrt(3.0) / 2.0
SWEEPS = 4
G = 8
T = 64
L = 128
Q = 4
C = 3
WIDE = Q * C * L
BLOCK = C * L
LO, MID, HI = 0, 5, 15
EXT = 18
FORTH = ((0, 3), (3, 1))
BACK = ((0, 1), (1, 2), (3, 1))
FAR = ((2, 1), (2, 0), (1, 1), (3, 1), (1, 0), (3, 0), (0, 1))


def tables():
    n = np.arange(T)
    forward = np.zeros((T, T))
    inverse = np.zeros((T, T))
    lam = np.zeros((2, T))
    beta = math.exp(math.log(ALPHA) / T)
    grow = ALPHA ** (n / T)
    for d in range(G):
        for half in range(2):
            for j in range(4):
                slot = 4 * d + j
                row = d * 8 + half * 4 + j
                if slot == 0:
                    freq, weight, part = 32 * half, 1.0, 0
                else:
                    freq, weight, part = slot, 2.0, half
                angle = 2.0 * math.pi * (freq * n % T) / T
                wave = np.cos(angle) if part == 0 else -np.sin(angle)
                forward[row] = wave * grow
                inverse[:, row] = weight * wave / grow / T
                lam[0, row] = 1.0 - beta * math.cos(2.0 * math.pi * freq / T)
                lam[1, row] = 0.0 if slot == 0 else beta * math.sin(2.0 * math.pi * freq / T)
    later = np.concatenate([forward[:, 8::8], np.zeros((T, 1))], axis=1)
    forward = np.concatenate([forward, later], axis=1)
    lam = np.broadcast_to(lam[:, :, None], (2, T, L))
    return [np.asarray(a, np.float32) for a in (forward, inverse, lam)]


def lanes(q, c):
    return pl.ds((q * C + c) * L, L)


def shift(tiles, step):
    lane = lax.broadcasted_iota(jnp.int32, (8, L), 1)
    turned = [pltpu.roll(t, step % L, axis=1) for t in tiles]
    edge = 0 if step == 1 else L - 1
    return [jnp.where(lane == edge, turned[(q - step) % Q], turned[q]) for q in range(Q)]


def permuted(tiles, order):
    out = []
    for q in range(Q):
        high = order[q] // L
        low = order[q] - high * L
        total = None
        for s in range(Q):
            part = jnp.take_along_axis(tiles[s], low, axis=1, mode="promise_in_bounds")
            total = part if total is None else jnp.where(high == s, part, total)
        out.append(total)
    return out


def couple(row, mid, low, up):
    s = HALF_ROOT
    h, u, v = range(3)
    diff = [[up[c][q] - low[c][q] for q in range(Q)] for c in range(3)]
    east = shift([mid[u][q] + 0.5 * low[u][q] - s * low[v][q] for q in range(Q)], -1)
    west = shift([mid[u][q] + 0.5 * up[u][q] - s * up[v][q] for q in range(Q)], 1)
    off_h = [east[q] - west[q] + 0.5 * diff[u][q] + s * diff[v][q] for q in range(Q)]
    low_m, up_p = shift(low[h], -1), shift(up[h], 1)
    mid_m, mid_p = shift(mid[h], -1), shift(mid[h], 1)
    off_u = [mid_m[q] - mid_p[q] + 0.5 * (diff[h][q] - up_p[q] + low_m[q]) for q in range(Q)]
    off_v = [s * (diff[h][q] + up_p[q] - low_m[q]) for q in range(Q)]
    return off_h, off_u, off_v


def load(ref, row):
    return [[ref[row, :, lanes(q, c)] for q in range(Q)] for c in range(C)]


def store(ref, row, tiles):
    for c in range(C):
        for q in range(Q):
            ref[row, :, lanes(q, c)] = tiles[c][q]


def wide(ref, q, i, row):
    return jnp.broadcast_to(ref[q, i, pl.ds(row, 1), :], (8, L))


def kernel(
    bands,
    it_any, fo_any, st_any, damp_any, cori_any, coup_any, order_any, fwd_any, inv_any, lam_any,
    out_ref,
    fwd_ref, inv_ref, lam_ref, it_v, fo_v, out_v, st_v, fixed,
    own_c, own_o, low_c, low_o, high_c, high_o, first,
    rows_t, halo_lo, halo_hi, coef, spec, cur,
    e_recv, a_send, a_recv, b_send, b_recv, c_send, c_recv, d_send, d_recv,
    in_sem, side_send, side_recv, e_ss, e_rs, a_ss, a_rs, b_ss, b_rs, c_ss, c_rs, d_ss, d_rs,
):
    me = lax.axis_index("tm")
    me_x, me_y = me // 2, lax.rem(me, 2)
    band = lax.axis_index("mesh")
    below = lax.rem(band + bands - 1, bands)
    above = lax.rem(band + 1, bands)
    peers = [lax.rem(me_x + dx, 4) * 2 + lax.rem(me_y + dy, 2) for dx, dy in FAR]

    def by_lanes(wide_ref, tiled_ref, base):
        return [
            pltpu.make_async_copy(wide_ref.at[:, :, pl.ds(q * L, L)], tiled_ref.at[q], in_sem.at[base + q])
            for q in range(Q)
        ]

    fields = by_lanes(it_any, it_v, 0)
    forces = by_lanes(fo_any, fo_v, 4)
    loads = [
        pltpu.make_async_copy(source, target, in_sem.at[8 + i])
        for i, (source, target) in enumerate(
            [
                (st_any, st_v), (damp_any, fixed.at[0]), (cori_any, fixed.at[1]), (coup_any, fixed.at[2]),
                (order_any, own_o), (fwd_any, fwd_ref), (inv_any, inv_ref), (lam_any, lam_ref),
            ]
        )
    ]
    for one in fields + forces + loads:
        one.start()
    barrier = pltpu.get_barrier_semaphore()
    for peer in peers:
        pl.semaphore_signal(barrier, 1, device_id={"tm": peer}, device_id_type=MESH)
    for p in (below, above):
        pl.semaphore_signal(barrier, 1, device_id={"mesh": p}, device_id_type=MESH)

    sent = []

    def remote(src, dst, ss, rs, device):
        one = pltpu.make_async_remote_copy(
            src_ref=src, dst_ref=dst, send_sem=ss, recv_sem=rs, device_id=device, device_id_type=MESH
        )
        sent.append(one)
        return one

    def side(index, src, dst, p):
        return remote(src, dst, side_send.at[index], side_recv.at[index], {"mesh": p})

    def hop(src, dst, ss, rs, groups, index):
        start, count = groups[index]
        part = pl.ds(start, count)
        return [
            remote(
                src.at[peer, part], dst.at[me, part],
                ss.at[index * 7 + k], rs.at[index * 7 + k], {"tm": peer},
            )
            for k, peer in enumerate(peers)
        ]

    def start(copies):
        for one in copies:
            one.start()

    def arrive(copies):
        for one in copies:
            one.wait_recv()

    def keep(src, dst, group):
        for m in range(group[0], group[0] + group[1]):
            dst[me, m] = src[me, m]

    for one in fields:
        one.wait()
    for r in range(8):
        for c in range(C):
            for q in range(Q):
                rows_t[r + 1, :, lanes(q, c)] = it_v[q, c, pl.ds(r, 8, stride=8), :]
    for one in loads + forces:
        one.wait()
    for q in range(Q):
        for i in range(3):
            own_c[q, i] = fixed[i, :, pl.ds(q * L, L)]
            first[q, i] = jnp.where(me == 0, st_v[i, :, pl.ds(q * L, L)], 0.0)

    sub = lax.broadcasted_iota(jnp.int32, (8, L), 0)

    def residual_row(r, half, m):
        mid = load(rows_t, r + 1)
        off = couple(r, mid, load(rows_t, r), load(rows_t, r + 2))
        for q in range(Q):
            damp, cori, coup = [wide(own_c, q, i, r) for i in range(3)]
            h, u, v = mid[0][q], mid[1][q], mid[2][q]
            applied = [damp * h, damp * u - cori * v, damp * v + cori * u]
            for c in range(C):
                before = jnp.where(sub == 0, wide(first, q, c, r), pltpu.roll(mid[c][q], 1, axis=0))
                force = fo_v[q, c, pl.ds(r, 8, stride=8), :]
                a_send[2 * q + half, m, :, pl.ds(c * L, L)] = (
                    force + before - mid[c][q] - (applied[c] + coup * off[c][q])
                )

    def residual_pair(m, _):
        residual_row(3 - m, 0, m)
        residual_row(4 + m, 1, m)
        return 0

    lax.fori_loop(0, 3, residual_pair, 0)

    pl.semaphore_wait(barrier, 9)
    halos = [side(0, rows_t.at[1], halo_hi, below), side(1, rows_t.at[8], halo_lo, above)]
    start(halos)
    last = pl.ds(T - 8, 8)
    hop_e = [
        remote(it_v.at[peer // 2, :, last, :], e_recv.at[me], e_ss.at[k], e_rs.at[k], {"tm": peer})
        for k, peer in enumerate(peers)
    ]
    start(hop_e)
    hop_a = [hop(a_send, a_recv, a_ss, a_rs, FORTH, i) for i in range(len(FORTH))]
    start(hop_a[0])
    params = [
        side(2, own_c, high_c, below), side(3, own_c, low_c, above),
        side(4, own_o, high_o, below), side(5, own_o, low_o, above),
    ]
    start(params)
    e_recv[me] = it_v[me_x, :, last, :]
    keep(a_send, a_recv, FORTH[0])

    def order(ref, which):
        return [jnp.broadcast_to(ref[pl.ds(which, 1), pl.ds(q * L, L)], (8, L)) for q in range(Q)]

    def halo(ref, row, which):
        tiles = [[ref[:, lanes(q, c)] for q in range(Q)] for c in range(C)]
        store(rows_t, row, [permuted(tiles[c], order(own_o, which)) for c in range(C)])

    arrive(halos)
    halo(halo_lo, 0, 0)
    halo(halo_hi, 9, 1)
    residual_pair(3, 0)
    start(hop_a[1])
    keep(a_send, a_recv, FORTH[1])

    lam_re = lam_ref[0, pl.ds(me * 8, 8), :]
    lam_im = lam_ref[1, pl.ds(me * 8, 8), :]
    sign = jnp.where(sub < 4, -1.0, 1.0)

    def coef_row(ref, offset):
        def body(r, _):
            for q in range(Q):
                damp, cori, coup = [wide(ref, q, i, r) for i in range(3)]
                a_re = lam_re + damp
                a_im = lam_im
                inv = 1.0 / (a_re * a_re + a_im * a_im)
                d_re = a_re * a_re - a_im * a_im + cori * cori
                d_im = 2.0 * a_re * a_im
                d_inv = 1.0 / (d_re * d_re + d_im * d_im)
                seven = [
                    a_re * inv,
                    -sign * a_im * inv,
                    (a_re * d_re + a_im * d_im) * d_inv,
                    sign * (a_im * d_re - a_re * d_im) * d_inv,
                    cori * d_re * d_inv,
                    -sign * cori * d_im * d_inv,
                    coup,
                ]
                for i in range(7):
                    coef[r + offset, i, :, pl.ds(q * L, L)] = seven[i]
            return 0

        return body

    lax.fori_loop(0, 8, coef_row(own_c, MID), 0)

    def transform(table, src, dst, m, extra):
        rows = src[:, m].reshape(T, BLOCK)
        if extra is not None:
            rows = jnp.concatenate([rows, extra], axis=0)
        dst[:, m] = jnp.dot(
            table, rows, precision=lax.Precision.HIGHEST, preferred_element_type=jnp.float32
        ).reshape(G, 8, BLOCK)

    def previous(m):
        row = 3 - m + me_y * (1 + 2 * m)
        return jnp.concatenate([e_flat(c, row) for c in range(C)], axis=1)

    def e_flat(c, row):
        return e_recv.reshape(G * C * 8, L)[pl.ds(c * 8 + row, G, stride=C * 8), :]

    arrive(hop_e)
    hop_b = [hop(b_send, b_recv, b_ss, b_rs, FORTH, i) for i in range(len(FORTH))]
    for i, (begin, count) in enumerate(FORTH):
        arrive(hop_a[i])
        for m in range(begin, begin + count):
            transform(fwd_ref[...], a_recv, b_send, m, previous(m))
        start(hop_b[i])
        keep(b_send, b_recv, FORTH[i])

    arrive(params)
    lax.fori_loop(5, 8, coef_row(low_c, LO - 5), 0)
    lax.fori_loop(0, 3, coef_row(high_c, HI), 0)

    def solve(row, x):
        out = [[], [], []]
        for q in range(Q):
            k = [coef[row, i, :, pl.ds(q * L, L)] for i in range(6)]
            xh, xu, xv = x[0][q], x[1][q], x[2][q]
            sh, su, sv = [pltpu.roll(t, 4, axis=0) for t in (xh, xu, xv)]
            out[0].append(k[0] * xh + k[1] * sh)
            out[1].append(k[2] * xu + k[3] * su + (k[4] * xv + k[5] * sv))
            out[2].append(k[2] * xv + k[3] * sv - (k[4] * xu + k[5] * su))
        return out

    def first_row(row):
        store(cur.at[0], row, solve(row, load(spec, row)))

    def sweep_row(level, row):
        src = cur.at[level]
        off = couple(row, load(src, row), load(src, row - 1), load(src, row + 1))
        full = load(spec, row)
        x = [
            [full[c][q] - coef[row, 6, :, pl.ds(q * L, L)] * off[c][q] for q in range(Q)]
            for c in range(C)
        ]
        return solve(row, x)

    def sweep_pair(level, low, high):
        def body(i, _):
            store(cur.at[level + 1], low + i, sweep_row(level, low + i))
            store(cur.at[level + 1], high - i, sweep_row(level, high - i))
            return 0

        return body

    def ghost(level, to, source, ref, which):
        src = cur.at[level]
        tiles = load(src, source)
        store(src, to, [permuted(tiles[c], order(ref, which)) for c in range(C)])

    def own_rows(m, _):
        for half, r in ((0, 3 - m), (1, 4 + m)):
            for q in range(Q):
                for c in range(C):
                    spec[MID + r, :, lanes(q, c)] = b_recv[2 * q + half, m, :, pl.ds(c * L, L)]
        return 0

    def own_first(m, _):
        first_row(MID + 3 - m)
        first_row(MID + 4 + m)
        return 0

    def rim(index, src, dst, count, p):
        return side(index, spec.at[pl.ds(src, count)], spec.at[pl.ds(dst, count)], p)

    rims = [
        rim(6, MID + 1, HI + 1, 2, below), rim(7, MID + 5, LO, 2, above),
        rim(8, MID, HI, 1, below), rim(9, MID + 7, LO + 2, 1, above),
    ]
    arrive(hop_b[0])
    lax.fori_loop(0, 3, own_rows, 0)
    start(rims[:2])
    lax.fori_loop(0, 3, own_first, 0)
    lax.fori_loop(0, 2, sweep_pair(0, MID + 2, MID + 5), 0)
    arrive(hop_b[1])
    own_rows(3, 0)
    start(rims[2:])
    own_first(3, 0)
    ghost(0, LO + 3, MID, low_o, 1)
    ghost(0, HI - 1, MID + 7, high_o, 0)
    lax.fori_loop(0, 1, sweep_pair(0, MID + 1, MID + 6), 0)
    lax.fori_loop(0, 2, sweep_pair(1, MID + 2, MID + 5), 0)

    hop_c = [hop(c_send, c_recv, c_ss, c_rs, BACK, i) for i in range(len(BACK))]

    def last_pair(m):
        for half, r in ((0, 3 - m), (1, 4 + m)):
            tiles = sweep_row(2, MID + r)
            for q in range(Q):
                for c in range(C):
                    c_send[2 * q + half, m, :, pl.ds(c * L, L)] = tiles[c][q]

    def finish(i):
        begin, count = BACK[i]
        if count == 1:
            last_pair(begin)
        else:
            def body(m, _):
                last_pair(m)
                return 0

            lax.fori_loop(begin, begin + count, body, 0)
        start(hop_c[i])
        keep(c_send, c_recv, BACK[i])

    finish(0)
    arrive(rims)

    def rim_first(i, _):
        first_row(LO + i)
        first_row(HI + 2 - i)
        return 0

    lax.fori_loop(0, 3, rim_first, 0)
    ghost(0, MID - 1, LO + 2, own_o, 0)
    ghost(0, MID + 8, HI, own_o, 1)
    lax.fori_loop(0, 2, sweep_pair(0, LO + 1, HI + 1), 0)
    lax.fori_loop(0, 1, sweep_pair(0, MID, MID + 7), 0)
    ghost(1, LO + 3, MID, low_o, 1)
    ghost(1, HI - 1, MID + 7, high_o, 0)
    ghost(1, MID - 1, LO + 2, own_o, 0)
    ghost(1, MID + 8, HI, own_o, 1)
    lax.fori_loop(0, 1, sweep_pair(1, LO + 2, HI), 0)
    lax.fori_loop(0, 2, sweep_pair(1, MID, MID + 7), 0)
    ghost(2, MID - 1, LO + 2, own_o, 0)
    ghost(2, MID + 8, HI, own_o, 1)
    for i in range(1, len(BACK)):
        finish(i)

    hop_d = [hop(d_send, d_recv, d_ss, d_rs, BACK, i) for i in range(len(BACK))]
    for i, (begin, count) in enumerate(BACK):
        arrive(hop_c[i])
        for m in range(begin, begin + count):
            transform(inv_ref[...], c_recv, d_send, m, None)
        start(hop_d[i])
        keep(d_send, d_recv, BACK[i])
    for i, (begin, count) in enumerate(BACK):
        arrive(hop_d[i])
        for m in range(begin, begin + count):
            for half, r in ((0, 3 - m), (1, 4 + m)):
                for q in range(Q):
                    for c in range(C):
                        out_v[q, c, pl.ds(r, 8, stride=8), :] = (
                            rows_t[r + 1, :, lanes(q, c)] + d_recv[2 * q + half, m, :, pl.ds(c * L, L)]
                        )
    for q in range(Q):
        for c in range(C):
            out_ref[c, :, pl.ds(q * L, L)] = out_v[q, c]
    for one in sent:
        one.wait_send()


def on_device(bands, iterate, forcing, start_state, damping, coriolis, coupling, edge_order):
    forward, inverse, lam = tables()
    flat = (C, T, Q * L)
    hbm = pl.BlockSpec(memory_space=pltpu.HBM)
    f32, i32 = jnp.float32, jnp.int32
    block = pltpu.VMEM((G, 4, 8, BLOCK), f32)
    staged = pltpu.VMEM((3, 8, Q * L), f32)
    own, pair = pltpu.VMEM((Q, 3, 8, L), f32), pltpu.VMEM((2, Q * L), i32)
    tiled = pltpu.VMEM((Q, C, T, L), f32)
    row = pltpu.VMEM((8, WIDE), f32)
    dma = pltpu.SemaphoreType.DMA
    out = pl.pallas_call(
        functools.partial(kernel, bands),
        out_shape=pltpu.VMEM(flat, f32),
        in_specs=[hbm] * 10,
        out_specs=pl.BlockSpec(memory_space=pltpu.VMEM),
        scratch_shapes=[
            pltpu.VMEM((T, T + 8), f32), pltpu.VMEM((T, T), f32), pltpu.VMEM((2, T, L), f32),
            tiled, tiled, tiled, staged, staged,
            own, pair, own, pair, own, pair, own,
            pltpu.VMEM((10, 8, WIDE), f32), row, row,
            pltpu.VMEM((EXT, 7, 8, Q * L), f32),
            pltpu.VMEM((EXT, 8, WIDE), f32),
            pltpu.VMEM((SWEEPS, EXT, 8, WIDE), f32),
            pltpu.VMEM((G, C, 8, L), f32),
        ]
        + [block] * 8
        + [dma((16,)), dma((10,)), dma((10,)), dma((7,)), dma((7,))]
        + [dma((7 * len(FORTH),))] * 4
        + [dma((7 * len(BACK),))] * 4,
        compiler_params=pltpu.CompilerParams(
            collective_id=0, has_side_effects=True, vmem_limit_bytes=40 * 1024 * 1024
        ),
    )(
        *[
            pltpu.with_memory_space_constraint(jnp.asarray(x), pltpu.HBM)
            for x in (
                iterate.reshape(flat), forcing.reshape(flat), start_state, damping, coriolis, coupling,
                edge_order.reshape(2, Q * L), forward, inverse, lam,
            )
        ]
    )
    return out.reshape(iterate.shape)


def solution(mesh):
    in_specs = (
        P(None, "tm", "mesh", None),
        P(None, "tm", "mesh", None),
        P(None, "mesh", None),
        P("mesh", None),
        P("mesh", None),
        P("mesh", None),
        P("mesh", None, None),
    )
    return jax.shard_map(
        functools.partial(on_device, mesh.shape["mesh"]),
        mesh=mesh, in_specs=in_specs, out_specs=P(None, "tm", "mesh", None), check_vma=False,
    )
```

```python
import functools
import math

import jax
import jax.numpy as jnp
import numpy as np
from jax import lax
from jax.experimental import pallas as pl
from jax.experimental.pallas import tpu as pltpu
from jax.sharding import PartitionSpec as P

MESH = pl.DeviceIdType.MESH
ALPHA = 0.1
HALF_ROOT = math.sqrt(3.0) / 2.0
SWEEPS = 4
G = 8
T = 64
L = 128
Q = 4
C = 3
WIDE = Q * C * L
BLOCK = C * L
LO, MID, HI = 0, 5, 15
EXT = 18
FORTH = ((0, 3), (3, 1))
BACK = ((0, 1), (1, 2), (3, 1))
UNROLL = True
FAR = ((2, 1), (2, 0), (1, 1), (3, 1), (1, 0), (3, 0), (0, 1))


def tables():
    n = np.arange(T)
    forward = np.zeros((T, T))
    inverse = np.zeros((T, T))
    lam = np.zeros((2, T))
    beta = math.exp(math.log(ALPHA) / T)
    grow = ALPHA ** (n / T)
    for d in range(G):
        for half in range(2):
            for j in range(4):
                slot = 4 * d + j
                row = d * 8 + half * 4 + j
                if slot == 0:
                    freq, weight, part = 32 * half, 1.0, 0
                else:
                    freq, weight, part = slot, 2.0, half
                angle = 2.0 * math.pi * (freq * n % T) / T
                wave = np.cos(angle) if part == 0 else -np.sin(angle)
                forward[row] = wave * grow
                inverse[:, row] = weight * wave / grow / T
                lam[0, row] = 1.0 - beta * math.cos(2.0 * math.pi * freq / T)
                lam[1, row] = 0.0 if slot == 0 else beta * math.sin(2.0 * math.pi * freq / T)
    later = np.concatenate([forward[:, 8::8], np.zeros((T, 1))], axis=1)
    forward = np.concatenate([forward, later], axis=1)
    lam = np.broadcast_to(lam[:, :, None], (2, T, L))
    return [np.asarray(a, np.float32) for a in (forward, inverse, lam)]


def lanes(q, c):
    return pl.ds((q * C + c) * L, L)


def shift(tiles, step):
    lane = lax.broadcasted_iota(jnp.int32, (8, L), 1)
    turned = [pltpu.roll(t, step % L, axis=1) for t in tiles]
    edge = 0 if step == 1 else L - 1
    return [jnp.where(lane == edge, turned[(q - step) % Q], turned[q]) for q in range(Q)]


def permuted(tiles, order):
    out = []
    for q in range(Q):
        high = order[q] // L
        low = order[q] - high * L
        total = None
        for s in range(Q):
            part = jnp.take_along_axis(tiles[s], low, axis=1, mode="promise_in_bounds")
            total = part if total is None else jnp.where(high == s, part, total)
        out.append(total)
    return out


def couple(row, mid, low, up):
    s = HALF_ROOT
    h, u, v = range(3)
    diff = [[up[c][q] - low[c][q] for q in range(Q)] for c in range(3)]
    east = shift([mid[u][q] + 0.5 * low[u][q] - s * low[v][q] for q in range(Q)], -1)
    west = shift([mid[u][q] + 0.5 * up[u][q] - s * up[v][q] for q in range(Q)], 1)
    off_h = [east[q] - west[q] + 0.5 * diff[u][q] + s * diff[v][q] for q in range(Q)]
    low_m, up_p = shift(low[h], -1), shift(up[h], 1)
    mid_m, mid_p = shift(mid[h], -1), shift(mid[h], 1)
    off_u = [mid_m[q] - mid_p[q] + 0.5 * (diff[h][q] - up_p[q] + low_m[q]) for q in range(Q)]
    off_v = [s * (diff[h][q] + up_p[q] - low_m[q]) for q in range(Q)]
    return off_h, off_u, off_v


def load(ref, row):
    return [[ref[row, :, lanes(q, c)] for q in range(Q)] for c in range(C)]


def store(ref, row, tiles):
    for c in range(C):
        for q in range(Q):
            ref[row, :, lanes(q, c)] = tiles[c][q]


def wide(ref, q, i, row):
    return jnp.broadcast_to(ref[q, i, pl.ds(row, 1), :], (8, L))


def kernel(
    bands,
    it_any, fo_any, st_any, damp_any, cori_any, coup_any, order_any, fwd_any, inv_any, lam_any,
    out_ref,
    fwd_ref, inv_ref, lam_ref, it_v, fo_v, out_v, st_v, fixed,
    own_c, own_o, low_c, low_o, high_c, high_o, first,
    rows_t, halo_lo, halo_hi, coef, spec, cur,
    e_recv, a_send, a_recv, b_send, b_recv, c_send, c_recv, d_send, d_recv,
    in_sem, side_send, side_recv, e_ss, e_rs, a_ss, a_rs, b_ss, b_rs, c_ss, c_rs, d_ss, d_rs,
):
    me = lax.axis_index("tm")
    me_x, me_y = me // 2, lax.rem(me, 2)
    band = lax.axis_index("mesh")
    below = lax.rem(band + bands - 1, bands)
    above = lax.rem(band + 1, bands)
    peers = [lax.rem(me_x + dx, 4) * 2 + lax.rem(me_y + dy, 2) for dx, dy in FAR]

    barrier = pltpu.get_barrier_semaphore()
    for p in (below, above):
        pl.semaphore_signal(barrier, 1, device_id={"mesh": p}, device_id_type=MESH)
    for peer in peers:
        pl.semaphore_signal(barrier, 1, device_id={"tm": peer}, device_id_type=MESH)

    def by_lanes(wide_ref, tiled_ref, base):
        return [
            pltpu.make_async_copy(wide_ref.at[:, :, pl.ds(q * L, L)], tiled_ref.at[q], in_sem.at[base + q])
            for q in range(Q)
        ]

    fields = by_lanes(it_any, it_v, 0)
    forces = by_lanes(fo_any, fo_v, 4)
    loads = [
        pltpu.make_async_copy(source, target, in_sem.at[8 + i])
        for i, (source, target) in enumerate(
            [
                (st_any, st_v), (damp_any, fixed.at[0]), (cori_any, fixed.at[1]), (coup_any, fixed.at[2]),
                (order_any, own_o), (fwd_any, fwd_ref), (inv_any, inv_ref), (lam_any, lam_ref),
            ]
        )
    ]

    for one in fields + forces + loads:
        one.start()
    sent = []

    def remote(src, dst, ss, rs, device):
        one = pltpu.make_async_remote_copy(
            src_ref=src, dst_ref=dst, send_sem=ss, recv_sem=rs, device_id=device, device_id_type=MESH
        )
        sent.append(one)
        return one

    def side(index, src, dst, p):
        return remote(src, dst, side_send.at[index], side_recv.at[index], {"mesh": p})

    class Hop:
        def __init__(self, src, dst, ss, rs, groups, index):
            part, base = pl.ds(*groups[index]), index * G

            def copy(peer):
                return pltpu.make_async_remote_copy(
                    src_ref=src.at[peer, part], dst_ref=dst.at[me, part],
                    send_sem=ss.at[base + peer], recv_sem=rs.at[base + peer],
                    device_id={"tm": peer}, device_id_type=MESH,
                )

            def out(peer):
                return pltpu.make_async_remote_copy(
                    src_ref=src.at[peer, part], dst_ref=dst.at[me, part],
                    send_sem=ss.at[base + peer], recv_sem=rs.at[base + me],
                    device_id={"tm": peer}, device_id_type=MESH,
                )

            self.copy, self.out = copy, out

        def half(self, half, act):
            for dx in (2, 1, 3):
                act(lax.rem(me_x + dx, 4) * 2 + half)
            pl.when(me_y != half)(lambda: act(me_x * 2 + half))

        def start(self):
            for peer in peers:
                self.out(peer).start()

        def arrive(self):
            for peer in peers:
                self.copy(peer).wait_recv()

        def start_half(self, half):
            self.half(half, lambda peer: self.out(peer).start())

        def arrive_half(self, half):
            self.half(half, lambda peer: self.copy(peer).wait_recv())

        def sent(self):
            for peer in peers:
                self.copy(peer).wait_send()

    def hops(src, dst, ss, rs, groups):
        return [Hop(src, dst, ss, rs, groups, i) for i in range(len(groups))]

    def start(copies):
        for one in copies:
            one.start()

    def arrive(copies):
        for one in copies:
            one.wait_recv()

    def keep(src, dst, group):
        for m in range(group[0], group[0] + group[1]):
            dst[me, m] = src[me, m]

    for one in fields:
        one.wait()
    for r in range(8):
        for c in range(C):
            for q in range(Q):
                rows_t[r + 1, :, lanes(q, c)] = it_v[q, c, pl.ds(r, 8, stride=8), :]
    for one in loads + forces:
        one.wait()
    for q in range(Q):
        for i in range(3):
            own_c[q, i] = fixed[i, :, pl.ds(q * L, L)]
            first[q, i] = jnp.where(me == 0, st_v[i, :, pl.ds(q * L, L)], 0.0)

    sub = lax.broadcasted_iota(jnp.int32, (8, L), 0)

    def residual_row(r, half, m):
        mid = load(rows_t, r + 1)
        off = couple(r, mid, load(rows_t, r), load(rows_t, r + 2))
        for q in range(Q):
            damp, cori, coup = [wide(own_c, q, i, r) for i in range(3)]
            h, u, v = mid[0][q], mid[1][q], mid[2][q]
            applied = [damp * h, damp * u - cori * v, damp * v + cori * u]
            for c in range(C):
                before = jnp.where(sub == 0, wide(first, q, c, r), pltpu.roll(mid[c][q], 1, axis=0))
                force = fo_v[q, c, pl.ds(r, 8, stride=8), :]
                a_send[2 * q + half, m, :, pl.ds(c * L, L)] = (
                    force + before - mid[c][q] - (applied[c] + coup * off[c][q])
                )

    def residual_pair(m, _):
        residual_row(3 - m, 0, m)
        residual_row(4 + m, 1, m)
        return 0

    lax.fori_loop(0, 3, residual_pair, 0)

    pl.semaphore_wait(barrier, 9)
    halos = [side(0, rows_t.at[1], halo_hi, below), side(1, rows_t.at[8], halo_lo, above)]
    start(halos)
    last = pl.ds(T - 8, 8)
    hop_e = [
        remote(it_v.at[peer // 2, :, last, :], e_recv.at[me], e_ss.at[k], e_rs.at[k], {"tm": peer})
        for k, peer in enumerate(peers)
    ]
    start(hop_e)
    hop_a = hops(a_send, a_recv, a_ss, a_rs, FORTH)
    hop_a[0].start()
    params = [
        side(2, own_c, high_c, below), side(3, own_c, low_c, above),
        side(4, own_o, high_o, below), side(5, own_o, low_o, above),
    ]
    start(params)
    e_recv[me] = it_v[me_x, :, last, :]
    keep(a_send, a_recv, FORTH[0])

    def order(ref, which):
        return [jnp.broadcast_to(ref[pl.ds(which, 1), pl.ds(q * L, L)], (8, L)) for q in range(Q)]

    def halo(ref, row, which):
        tiles = [[ref[:, lanes(q, c)] for q in range(Q)] for c in range(C)]
        store(rows_t, row, [permuted(tiles[c], order(own_o, which)) for c in range(C)])

    arrive(halos[:1])
    halo(halo_hi, 9, 1)
    residual_row(7, 1, 3)
    hop_a[1].start_half(1)
    arrive(halos[1:])
    halo(halo_lo, 0, 0)
    residual_row(0, 0, 3)
    hop_a[1].start_half(0)
    keep(a_send, a_recv, FORTH[1])

    lam_re = lam_ref[0, pl.ds(me * 8, 8), :]
    lam_im = lam_ref[1, pl.ds(me * 8, 8), :]
    sign = jnp.where(sub < 4, -1.0, 1.0)

    def coef_row(ref, offset):
        def body(r, _):
            for q in range(Q):
                damp, cori, coup = [wide(ref, q, i, r) for i in range(3)]
                a_re = lam_re + damp
                a_im = lam_im
                inv = 1.0 / (a_re * a_re + a_im * a_im)
                d_re = a_re * a_re - a_im * a_im + cori * cori
                d_im = 2.0 * a_re * a_im
                d_inv = 1.0 / (d_re * d_re + d_im * d_im)
                seven = [
                    a_re * inv,
                    -sign * a_im * inv,
                    (a_re * d_re + a_im * d_im) * d_inv,
                    sign * (a_im * d_re - a_re * d_im) * d_inv,
                    cori * d_re * d_inv,
                    -sign * cori * d_im * d_inv,
                    coup,
                ]
                for i in range(7):
                    coef[r + offset, i, :, pl.ds(q * L, L)] = seven[i]
            return 0

        return body

    lax.fori_loop(0, 8, coef_row(own_c, MID), 0)

    def transform(table, src, dst, m, extra):
        rows = src[:, m].reshape(T, BLOCK)
        if extra is not None:
            rows = jnp.concatenate([rows, extra], axis=0)
        dst[:, m] = jnp.dot(
            table, rows, precision=lax.Precision.HIGHEST, preferred_element_type=jnp.float32
        ).reshape(G, 8, BLOCK)

    def previous(m):
        row = 3 - m + me_y * (1 + 2 * m)
        return jnp.concatenate([e_flat(c, row) for c in range(C)], axis=1)

    def e_flat(c, row):
        return e_recv.reshape(G * C * 8, L)[pl.ds(c * 8 + row, G, stride=C * 8), :]

    arrive(hop_e)
    hop_b = hops(b_send, b_recv, b_ss, b_rs, FORTH)
    for i, (begin, count) in enumerate(FORTH):
        hop_a[i].arrive()
        for m in range(begin, begin + count):
            transform(fwd_ref[...], a_recv, b_send, m, previous(m))
        hop_b[i].start()
        keep(b_send, b_recv, FORTH[i])

    arrive(params)
    lax.fori_loop(5, 8, coef_row(low_c, LO - 5), 0)
    lax.fori_loop(0, 3, coef_row(high_c, HI), 0)

    def solve(row, x):
        out = [[], [], []]
        for q in range(Q):
            k = [coef[row, i, :, pl.ds(q * L, L)] for i in range(6)]
            xh, xu, xv = x[0][q], x[1][q], x[2][q]
            sh, su, sv = [pltpu.roll(t, 4, axis=0) for t in (xh, xu, xv)]
            out[0].append(k[0] * xh + k[1] * sh)
            out[1].append(k[2] * xu + k[3] * su + (k[4] * xv + k[5] * sv))
            out[2].append(k[2] * xv + k[3] * sv - (k[4] * xu + k[5] * su))
        return out

    def first_row(row):
        store(cur.at[0], row, solve(row, load(spec, row)))

    def sweep_row(level, row):
        src = cur.at[level]
        off = couple(row, load(src, row), load(src, row - 1), load(src, row + 1))
        full = load(spec, row)
        x = [
            [full[c][q] - coef[row, 6, :, pl.ds(q * L, L)] * off[c][q] for q in range(Q)]
            for c in range(C)
        ]
        return solve(row, x)

    def sweep_pair(level, low, high):
        def body(i, _):
            store(cur.at[level + 1], low + i, sweep_row(level, low + i))
            store(cur.at[level + 1], high - i, sweep_row(level, high - i))
            return 0

        return body

    def ghost(level, to, source, ref, which):
        src = cur.at[level]
        tiles = load(src, source)
        store(src, to, [permuted(tiles[c], order(ref, which)) for c in range(C)])

    def own_row(half, m):
        r = 4 + m if half else 3 - m
        for q in range(Q):
            for c in range(C):
                spec[MID + r, :, lanes(q, c)] = b_recv[2 * q + half, m, :, pl.ds(c * L, L)]

    def own_rows(m, _):
        own_row(0, m)
        own_row(1, m)
        return 0

    def own_first(m, _):
        first_row(MID + 3 - m)
        first_row(MID + 4 + m)
        return 0

    def rim(index, src, dst, count, p):
        return side(index, spec.at[pl.ds(src, count)], spec.at[pl.ds(dst, count)], p)

    rims = [
        rim(6, MID + 1, HI + 1, 2, below), rim(7, MID, HI, 1, below),
        rim(8, MID + 5, LO, 2, above), rim(9, MID + 7, LO + 2, 1, above),
    ]
    hop_b[0].arrive()
    lax.fori_loop(0, 3, own_rows, 0)
    start([rims[0], rims[2]])
    lax.fori_loop(0, 3, own_first, 0)
    lax.fori_loop(0, 2, sweep_pair(0, MID + 2, MID + 5), 0)
    hop_b[1].arrive_half(1)
    own_row(1, 3)
    start(rims[3:])
    hop_b[1].arrive_half(0)
    own_row(0, 3)
    start(rims[1:2])
    own_first(3, 0)
    ghost(0, LO + 3, MID, low_o, 1)
    ghost(0, HI - 1, MID + 7, high_o, 0)
    lax.fori_loop(0, 1, sweep_pair(0, MID + 1, MID + 6), 0)
    lax.fori_loop(0, 2, sweep_pair(1, MID + 2, MID + 5), 0)

    hop_c = hops(c_send, c_recv, c_ss, c_rs, BACK)

    def last_row(half, m):
        tiles = sweep_row(2, MID + (4 + m if half else 3 - m))
        for q in range(Q):
            for c in range(C):
                c_send[2 * q + half, m, :, pl.ds(c * L, L)] = tiles[c][q]

    def sweep_rows(level, first_one):
        def body(i, _):
            store(cur.at[level + 1], first_one + i, sweep_row(level, first_one + i))
            return 0

        lax.fori_loop(0, 2, body, 0, unroll=UNROLL)

    def rim_first(first_one):
        def body(i, _):
            first_row(first_one + i)
            return 0

        lax.fori_loop(0, 3, body, 0)

    def finish(half, i):
        begin, count = BACK[i]

        def body(m, _):
            last_row(half, m)
            return 0

        lax.fori_loop(begin, begin + count, body, 0, unroll=UNROLL)
        hop_c[i].start_half(half)

    last_row(0, 0)
    last_row(1, 0)
    hop_c[0].start()
    arrive(rims[:2])
    rim_first(HI)
    ghost(0, MID + 8, HI, own_o, 1)
    sweep_rows(0, HI)
    store(cur.at[1], MID + 7, sweep_row(0, MID + 7))
    ghost(1, HI - 1, MID + 7, high_o, 0)
    ghost(1, MID + 8, HI, own_o, 1)
    store(cur.at[2], HI, sweep_row(1, HI))
    sweep_rows(1, MID + 6)
    ghost(2, MID + 8, HI, own_o, 1)
    for i in range(1, len(BACK)):
        finish(1, i)
    arrive(rims[2:])
    rim_first(LO)
    ghost(0, MID - 1, LO + 2, own_o, 0)
    sweep_rows(0, LO + 1)
    store(cur.at[1], MID, sweep_row(0, MID))
    ghost(1, LO + 3, MID, low_o, 1)
    ghost(1, MID - 1, LO + 2, own_o, 0)
    store(cur.at[2], LO + 2, sweep_row(1, LO + 2))
    sweep_rows(1, MID)
    ghost(2, MID - 1, LO + 2, own_o, 0)
    for i in range(1, len(BACK)):
        finish(0, i)
    for group in BACK:
        keep(c_send, c_recv, group)

    hop_d = hops(d_send, d_recv, d_ss, d_rs, BACK)
    for i, (begin, count) in enumerate(BACK):
        hop_c[i].arrive()
        for m in range(begin, begin + count):
            transform(inv_ref[...], c_recv, d_send, m, None)
        hop_d[i].start()
        keep(d_send, d_recv, BACK[i])
    for half in (1, 0):
        for i, (begin, count) in enumerate(BACK):
            hop_d[i].arrive_half(half)
            for m in range(begin, begin + count):
                r = 4 + m if half else 3 - m
                for q in range(Q):
                    for c in range(C):
                        out_v[q, c, pl.ds(r, 8, stride=8), :] = (
                            rows_t[r + 1, :, lanes(q, c)] + d_recv[2 * q + half, m, :, pl.ds(c * L, L)]
                        )
    for q in range(Q):
        for c in range(C):
            out_ref[c, :, pl.ds(q * L, L)] = out_v[q, c]
    for one in sent:
        one.wait_send()
    for one in hop_a + hop_b + hop_c + hop_d:
        one.sent()


def on_device(bands, iterate, forcing, start_state, damping, coriolis, coupling, edge_order):
    forward, inverse, lam = tables()
    flat = (C, T, Q * L)
    hbm = pl.BlockSpec(memory_space=pltpu.HBM)
    f32, i32 = jnp.float32, jnp.int32
    block = pltpu.VMEM((G, 4, 8, BLOCK), f32)
    staged = pltpu.VMEM((3, 8, Q * L), f32)
    own, pair = pltpu.VMEM((Q, 3, 8, L), f32), pltpu.VMEM((2, Q * L), i32)
    tiled = pltpu.VMEM((Q, C, T, L), f32)
    row = pltpu.VMEM((8, WIDE), f32)
    dma = pltpu.SemaphoreType.DMA
    out = pl.pallas_call(
        functools.partial(kernel, bands),
        out_shape=pltpu.VMEM(flat, f32),
        in_specs=[hbm] * 10,
        out_specs=pl.BlockSpec(memory_space=pltpu.VMEM),
        scratch_shapes=[
            pltpu.VMEM((T, T + 8), f32), pltpu.VMEM((T, T), f32), pltpu.VMEM((2, T, L), f32),
            tiled, tiled, tiled, staged, staged,
            own, pair, own, pair, own, pair, own,
            pltpu.VMEM((10, 8, WIDE), f32), row, row,
            pltpu.VMEM((EXT, 7, 8, Q * L), f32),
            pltpu.VMEM((EXT, 8, WIDE), f32),
            pltpu.VMEM((SWEEPS, EXT, 8, WIDE), f32),
            pltpu.VMEM((G, C, 8, L), f32),
        ]
        + [block] * 8
        + [dma((16,)), dma((10,)), dma((10,)), dma((7,)), dma((7,))]
        + [dma((G * len(FORTH),))] * 4
        + [dma((G * len(BACK),))] * 4,
        compiler_params=pltpu.CompilerParams(
            collective_id=0, has_side_effects=True, vmem_limit_bytes=40 * 1024 * 1024
        ),
    )(
        *[
            pltpu.with_memory_space_constraint(jnp.asarray(x), pltpu.HBM)
            for x in (
                iterate.reshape(flat), forcing.reshape(flat), start_state, damping, coriolis, coupling,
                edge_order.reshape(2, Q * L), forward, inverse, lam,
            )
        ]
    )
    return out.reshape(iterate.shape)


def solution(mesh):
    in_specs = (
        P(None, "tm", "mesh", None),
        P(None, "tm", "mesh", None),
        P(None, "mesh", None),
        P("mesh", None),
        P("mesh", None),
        P("mesh", None),
        P("mesh", None, None),
    )
    return jax.shard_map(
        functools.partial(on_device, mesh.shape["mesh"]),
        mesh=mesh, in_specs=in_specs, out_specs=P(None, "tm", "mesh", None), check_vma=False,
    )
```

```python
import functools
import math

import jax
import jax.numpy as jnp
import numpy as np
from jax import lax
from jax.experimental import pallas as pl
from jax.experimental.pallas import tpu as pltpu
from jax.sharding import PartitionSpec as P

MESH = pl.DeviceIdType.MESH
ALPHA = 0.1
HALF_ROOT = math.sqrt(3.0) / 2.0
SWEEPS = 4
G = 8
T = 64
L = 128
Q = 4
C = 3
WIDE = Q * C * L
BLOCK = C * L
LO, MID, HI = 0, 5, 15
EXT = 18
FORTH = ((1, 2), (0, 1), (3, 1))
BACK = ((0, 1), (1, 2), (3, 1))
UNROLL = True
FAR = ((2, 1), (2, 0), (1, 1), (3, 1), (1, 0), (3, 0), (0, 1))


def tables():
    n = np.arange(T)
    forward = np.zeros((T, T))
    inverse = np.zeros((T, T))
    lam = np.zeros((2, T))
    beta = math.exp(math.log(ALPHA) / T)
    grow = ALPHA ** (n / T)
    for d in range(G):
        for half in range(2):
            for j in range(4):
                slot = 4 * d + j
                row = d * 8 + half * 4 + j
                if slot == 0:
                    freq, weight, part = 32 * half, 1.0, 0
                else:
                    freq, weight, part = slot, 2.0, half
                angle = 2.0 * math.pi * (freq * n % T) / T
                wave = np.cos(angle) if part == 0 else -np.sin(angle)
                forward[row] = wave * grow
                inverse[:, row] = weight * wave / grow / T
                lam[0, row] = 1.0 - beta * math.cos(2.0 * math.pi * freq / T)
                lam[1, row] = 0.0 if slot == 0 else beta * math.sin(2.0 * math.pi * freq / T)
    later = np.concatenate([forward[:, 8::8], np.zeros((T, 1))], axis=1)
    forward = np.concatenate([forward, later], axis=1)
    lam = np.broadcast_to(lam[:, :, None], (2, T, L))
    return [np.asarray(a, np.float32) for a in (forward, inverse, lam)]


def lanes(q, c):
    return pl.ds((q * C + c) * L, L)


def shift(tiles, step):
    lane = lax.broadcasted_iota(jnp.int32, (8, L), 1)
    turned = [pltpu.roll(t, step % L, axis=1) for t in tiles]
    edge = 0 if step == 1 else L - 1
    return [jnp.where(lane == edge, turned[(q - step) % Q], turned[q]) for q in range(Q)]


def permuted(tiles, order):
    out = []
    for q in range(Q):
        high = order[q] // L
        low = order[q] - high * L
        total = None
        for s in range(Q):
            part = jnp.take_along_axis(tiles[s], low, axis=1, mode="promise_in_bounds")
            total = part if total is None else jnp.where(high == s, part, total)
        out.append(total)
    return out


def couple(row, mid, low, up):
    s = HALF_ROOT
    h, u, v = range(3)
    diff = [[up[c][q] - low[c][q] for q in range(Q)] for c in range(3)]
    east = shift([mid[u][q] + 0.5 * low[u][q] - s * low[v][q] for q in range(Q)], -1)
    west = shift([mid[u][q] + 0.5 * up[u][q] - s * up[v][q] for q in range(Q)], 1)
    off_h = [east[q] - west[q] + 0.5 * diff[u][q] + s * diff[v][q] for q in range(Q)]
    low_m, up_p = shift(low[h], -1), shift(up[h], 1)
    mid_m, mid_p = shift(mid[h], -1), shift(mid[h], 1)
    off_u = [mid_m[q] - mid_p[q] + 0.5 * (diff[h][q] - up_p[q] + low_m[q]) for q in range(Q)]
    off_v = [s * (diff[h][q] + up_p[q] - low_m[q]) for q in range(Q)]
    return off_h, off_u, off_v


def load(ref, row):
    return [[ref[row, :, lanes(q, c)] for q in range(Q)] for c in range(C)]


def store(ref, row, tiles):
    for c in range(C):
        for q in range(Q):
            ref[row, :, lanes(q, c)] = tiles[c][q]


def wide(ref, q, i, row):
    return jnp.broadcast_to(ref[q, i, pl.ds(row, 1), :], (8, L))


def kernel(
    bands,
    it_any, fo_any, st_any, damp_any, cori_any, coup_any, order_any, fwd_any, inv_any, lam_any,
    out_ref,
    fwd_ref, inv_ref, lam_ref, it_v, fo_v, out_v, st_v, fixed,
    own_c, own_o, low_c, low_o, high_c, high_o, first,
    rows_t, halo_lo, halo_hi, coef, spec, cur,
    e_recv, a_send, a_recv, b_send, b_recv, c_send, c_recv, d_send, d_recv,
    in_sem, side_send, side_recv, e_ss, e_rs, a_ss, a_rs, b_ss, b_rs, c_ss, c_rs, d_ss, d_rs,
):
    me = lax.axis_index("tm")
    me_x, me_y = me // 2, lax.rem(me, 2)
    band = lax.axis_index("mesh")
    below = lax.rem(band + bands - 1, bands)
    above = lax.rem(band + 1, bands)
    peers = [lax.rem(me_x + dx, 4) * 2 + lax.rem(me_y + dy, 2) for dx, dy in FAR]

    barrier = pltpu.get_barrier_semaphore()
    for p in (below, above):
        pl.semaphore_signal(barrier, 1, device_id={"mesh": p}, device_id_type=MESH)
    for peer in peers:
        pl.semaphore_signal(barrier, 1, device_id={"tm": peer}, device_id_type=MESH)

    def by_lanes(wide_ref, tiled_ref, base):
        return [
            pltpu.make_async_copy(wide_ref.at[:, :, pl.ds(q * L, L)], tiled_ref.at[q], in_sem.at[base + q])
            for q in range(Q)
        ]

    fields = by_lanes(it_any, it_v, 0)
    forces = by_lanes(fo_any, fo_v, 4)
    loads = [
        pltpu.make_async_copy(source, target, in_sem.at[8 + i])
        for i, (source, target) in enumerate(
            [
                (st_any, st_v), (damp_any, fixed.at[0]), (cori_any, fixed.at[1]), (coup_any, fixed.at[2]),
                (order_any, own_o), (fwd_any, fwd_ref), (inv_any, inv_ref), (lam_any, lam_ref),
            ]
        )
    ]

    for one in fields + forces + loads:
        one.start()
    sent = []

    def remote(src, dst, ss, rs, device):
        one = pltpu.make_async_remote_copy(
            src_ref=src, dst_ref=dst, send_sem=ss, recv_sem=rs, device_id=device, device_id_type=MESH
        )
        sent.append(one)
        return one

    def side(index, src, dst, p):
        return remote(src, dst, side_send.at[index], side_recv.at[index], {"mesh": p})

    class Hop:
        def __init__(self, src, dst, ss, rs, groups, index):
            part, base = pl.ds(*groups[index]), index * G

            def copy(peer):
                return pltpu.make_async_remote_copy(
                    src_ref=src.at[peer, part], dst_ref=dst.at[me, part],
                    send_sem=ss.at[base + peer], recv_sem=rs.at[base + peer],
                    device_id={"tm": peer}, device_id_type=MESH,
                )

            def out(peer):
                return pltpu.make_async_remote_copy(
                    src_ref=src.at[peer, part], dst_ref=dst.at[me, part],
                    send_sem=ss.at[base + peer], recv_sem=rs.at[base + me],
                    device_id={"tm": peer}, device_id_type=MESH,
                )

            self.copy, self.out = copy, out

        def half(self, half, act):
            for dx in (2, 1, 3):
                act(lax.rem(me_x + dx, 4) * 2 + half)
            pl.when(me_y != half)(lambda: act(me_x * 2 + half))

        def start(self):
            for peer in peers:
                self.out(peer).start()

        def arrive(self):
            for peer in peers:
                self.copy(peer).wait_recv()

        def start_half(self, half):
            self.half(half, lambda peer: self.out(peer).start())

        def arrive_half(self, half):
            self.half(half, lambda peer: self.copy(peer).wait_recv())

        def sent(self):
            for peer in peers:
                self.copy(peer).wait_send()

    def hops(src, dst, ss, rs, groups):
        return [Hop(src, dst, ss, rs, groups, i) for i in range(len(groups))]

    def start(copies):
        for one in copies:
            one.start()

    def arrive(copies):
        for one in copies:
            one.wait_recv()

    def keep(src, dst, group):
        for m in range(group[0], group[0] + group[1]):
            dst[me, m] = src[me, m]

    for one in fields:
        one.wait()
    for r in range(8):
        for c in range(C):
            for q in range(Q):
                rows_t[r + 1, :, lanes(q, c)] = it_v[q, c, pl.ds(r, 8, stride=8), :]
    for one in loads + forces:
        one.wait()
    for q in range(Q):
        for i in range(3):
            own_c[q, i] = fixed[i, :, pl.ds(q * L, L)]
            first[q, i] = jnp.where(me == 0, st_v[i, :, pl.ds(q * L, L)], 0.0)

    sub = lax.broadcasted_iota(jnp.int32, (8, L), 0)

    def residual_row(r, half, m):
        mid = load(rows_t, r + 1)
        off = couple(r, mid, load(rows_t, r), load(rows_t, r + 2))
        for q in range(Q):
            damp, cori, coup = [wide(own_c, q, i, r) for i in range(3)]
            h, u, v = mid[0][q], mid[1][q], mid[2][q]
            applied = [damp * h, damp * u - cori * v, damp * v + cori * u]
            for c in range(C):
                before = jnp.where(sub == 0, wide(first, q, c, r), pltpu.roll(mid[c][q], 1, axis=0))
                force = fo_v[q, c, pl.ds(r, 8, stride=8), :]
                a_send[2 * q + half, m, :, pl.ds(c * L, L)] = (
                    force + before - mid[c][q] - (applied[c] + coup * off[c][q])
                )

    def residual_pair(m, _):
        residual_row(3 - m, 0, m)
        residual_row(4 + m, 1, m)
        return 0

    lax.fori_loop(1, 3, residual_pair, 0)
    residual_pair(0, 0)

    pl.semaphore_wait(barrier, 9)
    halos = [side(0, rows_t.at[1], halo_hi, below), side(1, rows_t.at[8], halo_lo, above)]
    start(halos)
    last = pl.ds(T - 8, 8)
    hop_e = [
        remote(it_v.at[peer // 2, :, last, :], e_recv.at[me], e_ss.at[k], e_rs.at[k], {"tm": peer})
        for k, peer in enumerate(peers)
    ]
    start(hop_e)
    hop_a = hops(a_send, a_recv, a_ss, a_rs, FORTH)
    hop_a[0].start()
    hop_a[1].start()
    params = [
        side(2, own_c, high_c, below), side(3, own_c, low_c, above),
        side(4, own_o, high_o, below), side(5, own_o, low_o, above),
    ]
    start(params)
    e_recv[me] = it_v[me_x, :, last, :]
    keep(a_send, a_recv, FORTH[0])
    keep(a_send, a_recv, FORTH[1])

    def order(ref, which):
        return [jnp.broadcast_to(ref[pl.ds(which, 1), pl.ds(q * L, L)], (8, L)) for q in range(Q)]

    def halo(ref, row, which):
        tiles = [[ref[:, lanes(q, c)] for q in range(Q)] for c in range(C)]
        store(rows_t, row, [permuted(tiles[c], order(own_o, which)) for c in range(C)])

    arrive(halos[:1])
    halo(halo_hi, 9, 1)
    residual_row(7, 1, 3)
    hop_a[2].start_half(1)
    arrive(halos[1:])
    halo(halo_lo, 0, 0)
    residual_row(0, 0, 3)
    hop_a[2].start_half(0)
    keep(a_send, a_recv, FORTH[2])

    lam_re = lam_ref[0, pl.ds(me * 8, 8), :]
    lam_im = lam_ref[1, pl.ds(me * 8, 8), :]
    sign = jnp.where(sub < 4, -1.0, 1.0)

    def coef_row(ref, offset):
        def body(r, _):
            for q in range(Q):
                damp, cori, coup = [wide(ref, q, i, r) for i in range(3)]
                a_re = lam_re + damp
                a_im = lam_im
                inv = 1.0 / (a_re * a_re + a_im * a_im)
                d_re = a_re * a_re - a_im * a_im + cori * cori
                d_im = 2.0 * a_re * a_im
                d_inv = 1.0 / (d_re * d_re + d_im * d_im)
                seven = [
                    a_re * inv,
                    -sign * a_im * inv,
                    (a_re * d_re + a_im * d_im) * d_inv,
                    sign * (a_im * d_re - a_re * d_im) * d_inv,
                    cori * d_re * d_inv,
                    -sign * cori * d_im * d_inv,
                    coup,
                ]
                for i in range(7):
                    coef[r + offset, i, :, pl.ds(q * L, L)] = seven[i]
            return 0

        return body

    lax.fori_loop(0, 8, coef_row(own_c, MID), 0)

    def transform(table, src, dst, m, extra):
        rows = src[:, m].reshape(T, BLOCK)
        if extra is not None:
            rows = jnp.concatenate([rows, extra], axis=0)
        dst[:, m] = jnp.dot(
            table, rows, precision=lax.Precision.HIGH, preferred_element_type=jnp.float32
        ).reshape(G, 8, BLOCK)

    def previous(m):
        row = 3 - m + me_y * (1 + 2 * m)
        return jnp.concatenate([e_flat(c, row) for c in range(C)], axis=1)

    def e_flat(c, row):
        return e_recv.reshape(G * C * 8, L)[pl.ds(c * 8 + row, G, stride=C * 8), :]

    arrive(hop_e)
    hop_b = hops(b_send, b_recv, b_ss, b_rs, FORTH)
    for i, (begin, count) in enumerate(FORTH):
        hop_a[i].arrive()
        for m in range(begin, begin + count):
            transform(fwd_ref[...], a_recv, b_send, m, previous(m))
        hop_b[i].start()
        keep(b_send, b_recv, FORTH[i])

    arrive(params)
    lax.fori_loop(5, 8, coef_row(low_c, LO - 5), 0)
    lax.fori_loop(0, 3, coef_row(high_c, HI), 0)

    def solve(row, x):
        out = [[], [], []]
        for q in range(Q):
            k = [coef[row, i, :, pl.ds(q * L, L)] for i in range(6)]
            xh, xu, xv = x[0][q], x[1][q], x[2][q]
            sh, su, sv = [pltpu.roll(t, 4, axis=0) for t in (xh, xu, xv)]
            out[0].append(k[0] * xh + k[1] * sh)
            out[1].append(k[2] * xu + k[3] * su + (k[4] * xv + k[5] * sv))
            out[2].append(k[2] * xv + k[3] * sv - (k[4] * xu + k[5] * su))
        return out

    def first_row(row):
        store(cur.at[0], row, solve(row, load(spec, row)))

    def sweep_row(level, row):
        src = cur.at[level]
        off = couple(row, load(src, row), load(src, row - 1), load(src, row + 1))
        full = load(spec, row)
        x = [
            [full[c][q] - coef[row, 6, :, pl.ds(q * L, L)] * off[c][q] for q in range(Q)]
            for c in range(C)
        ]
        return solve(row, x)

    def sweep_pair(level, low, high):
        def body(i, _):
            store(cur.at[level + 1], low + i, sweep_row(level, low + i))
            store(cur.at[level + 1], high - i, sweep_row(level, high - i))
            return 0

        return body

    def ghost(level, to, source, ref, which):
        src = cur.at[level]
        tiles = load(src, source)
        store(src, to, [permuted(tiles[c], order(ref, which)) for c in range(C)])

    def own_row(half, m):
        r = 4 + m if half else 3 - m
        for q in range(Q):
            for c in range(C):
                spec[MID + r, :, lanes(q, c)] = b_recv[2 * q + half, m, :, pl.ds(c * L, L)]

    def own_rows(m, _):
        own_row(0, m)
        own_row(1, m)
        return 0

    def own_first(m, _):
        first_row(MID + 3 - m)
        first_row(MID + 4 + m)
        return 0

    def rim(index, src, dst, count, p):
        return side(index, spec.at[pl.ds(src, count)], spec.at[pl.ds(dst, count)], p)

    rims = [
        rim(6, MID + 1, HI + 1, 2, below), rim(7, MID, HI, 1, below),
        rim(8, MID + 5, LO, 2, above), rim(9, MID + 7, LO + 2, 1, above),
    ]
    hop_b[0].arrive()
    lax.fori_loop(1, 3, own_rows, 0)
    start([rims[0], rims[2]])
    lax.fori_loop(1, 3, own_first, 0)
    hop_b[1].arrive()
    own_rows(0, 0)
    own_first(0, 0)
    lax.fori_loop(0, 2, sweep_pair(0, MID + 2, MID + 5), 0)
    hop_b[2].arrive_half(1)
    own_row(1, 3)
    start(rims[3:])
    hop_b[2].arrive_half(0)
    own_row(0, 3)
    start(rims[1:2])
    own_first(3, 0)
    ghost(0, LO + 3, MID, low_o, 1)
    ghost(0, HI - 1, MID + 7, high_o, 0)
    lax.fori_loop(0, 1, sweep_pair(0, MID + 1, MID + 6), 0)
    lax.fori_loop(0, 2, sweep_pair(1, MID + 2, MID + 5), 0)

    hop_c = hops(c_send, c_recv, c_ss, c_rs, BACK)

    def last_row(half, m):
        tiles = sweep_row(2, MID + (4 + m if half else 3 - m))
        for q in range(Q):
            for c in range(C):
                c_send[2 * q + half, m, :, pl.ds(c * L, L)] = tiles[c][q]

    def sweep_rows(level, first_one):
        def body(i, _):
            store(cur.at[level + 1], first_one + i, sweep_row(level, first_one + i))
            return 0

        lax.fori_loop(0, 2, body, 0, unroll=UNROLL)

    def rim_first(first_one):
        def body(i, _):
            first_row(first_one + i)
            return 0

        lax.fori_loop(0, 3, body, 0)

    def finish(half, i):
        begin, count = BACK[i]

        def body(m, _):
            last_row(half, m)
            return 0

        lax.fori_loop(begin, begin + count, body, 0, unroll=UNROLL)
        hop_c[i].start_half(half)

    last_row(0, 0)
    last_row(1, 0)
    hop_c[0].start()
    arrive(rims[:2])
    rim_first(HI)
    ghost(0, MID + 8, HI, own_o, 1)
    sweep_rows(0, HI)
    store(cur.at[1], MID + 7, sweep_row(0, MID + 7))
    ghost(1, HI - 1, MID + 7, high_o, 0)
    ghost(1, MID + 8, HI, own_o, 1)
    store(cur.at[2], HI, sweep_row(1, HI))
    sweep_rows(1, MID + 6)
    finish(1, 1)
    ghost(2, MID + 8, HI, own_o, 1)
    finish(1, 2)
    arrive(rims[2:3])
    first_row(LO)
    first_row(LO + 1)
    arrive(rims[3:])
    first_row(LO + 2)
    ghost(0, MID - 1, LO + 2, own_o, 0)
    sweep_rows(0, LO + 1)
    store(cur.at[1], MID, sweep_row(0, MID))
    ghost(1, LO + 3, MID, low_o, 1)
    ghost(1, MID - 1, LO + 2, own_o, 0)
    store(cur.at[2], LO + 2, sweep_row(1, LO + 2))
    sweep_rows(1, MID)
    finish(0, 1)
    ghost(2, MID - 1, LO + 2, own_o, 0)
    finish(0, 2)
    for group in BACK:
        keep(c_send, c_recv, group)

    for one in sent:
        one.wait_send()
    for one in hop_a + hop_b:
        one.sent()
    hop_d = hops(d_send, d_recv, d_ss, d_rs, BACK)
    for i, (begin, count) in enumerate(BACK):
        hop_c[i].arrive()
        for m in range(begin, begin + count):
            transform(inv_ref[...], c_recv, d_send, m, None)
        hop_d[i].start()
        keep(d_send, d_recv, BACK[i])
    for one in hop_c:
        one.sent()
    for half in (1, 0):
        for i, (begin, count) in enumerate(BACK):
            hop_d[i].arrive_half(half)
            for m in range(begin, begin + count):
                r = 4 + m if half else 3 - m
                for q in range(Q):
                    for c in range(C):
                        out_v[q, c, pl.ds(r, 8, stride=8), :] = (
                            rows_t[r + 1, :, lanes(q, c)] + d_recv[2 * q + half, m, :, pl.ds(c * L, L)]
                        )
    for q in range(Q):
        for c in range(C):
            out_ref[c, :, pl.ds(q * L, L)] = out_v[q, c]
    for one in hop_d:
        one.sent()


def on_device(bands, iterate, forcing, start_state, damping, coriolis, coupling, edge_order):
    forward, inverse, lam = tables()
    flat = (C, T, Q * L)
    hbm = pl.BlockSpec(memory_space=pltpu.HBM)
    f32, i32 = jnp.float32, jnp.int32
    block = pltpu.VMEM((G, 4, 8, BLOCK), f32)
    staged = pltpu.VMEM((3, 8, Q * L), f32)
    own, pair = pltpu.VMEM((Q, 3, 8, L), f32), pltpu.VMEM((2, Q * L), i32)
    tiled = pltpu.VMEM((Q, C, T, L), f32)
    row = pltpu.VMEM((8, WIDE), f32)
    dma = pltpu.SemaphoreType.DMA
    out = pl.pallas_call(
        functools.partial(kernel, bands),
        out_shape=pltpu.VMEM(flat, f32),
        in_specs=[hbm] * 10,
        out_specs=pl.BlockSpec(memory_space=pltpu.VMEM),
        scratch_shapes=[
            pltpu.VMEM((T, T + 8), f32), pltpu.VMEM((T, T), f32), pltpu.VMEM((2, T, L), f32),
            tiled, tiled, tiled, staged, staged,
            own, pair, own, pair, own, pair, own,
            pltpu.VMEM((10, 8, WIDE), f32), row, row,
            pltpu.VMEM((EXT, 7, 8, Q * L), f32),
            pltpu.VMEM((EXT, 8, WIDE), f32),
            pltpu.VMEM((SWEEPS, EXT, 8, WIDE), f32),
            pltpu.VMEM((G, C, 8, L), f32),
        ]
        + [block] * 8
        + [dma((16,)), dma((10,)), dma((10,)), dma((7,)), dma((7,))]
        + [dma((G * len(FORTH),))] * 4
        + [dma((G * len(BACK),))] * 4,
        compiler_params=pltpu.CompilerParams(
            collective_id=0, has_side_effects=True, vmem_limit_bytes=40 * 1024 * 1024
        ),
    )(
        *[
            pltpu.with_memory_space_constraint(jnp.asarray(x), pltpu.HBM)
            for x in (
                iterate.reshape(flat), forcing.reshape(flat), start_state, damping, coriolis, coupling,
                edge_order.reshape(2, Q * L), forward, inverse, lam,
            )
        ]
    )
    return out.reshape(iterate.shape)


def solution(mesh):
    in_specs = (
        P(None, "tm", "mesh", None),
        P(None, "tm", "mesh", None),
        P(None, "mesh", None),
        P("mesh", None),
        P("mesh", None),
        P("mesh", None),
        P("mesh", None, None),
    )
    return jax.shard_map(
        functools.partial(on_device, mesh.shape["mesh"]),
        mesh=mesh, in_specs=in_specs, out_specs=P(None, "tm", "mesh", None), check_vma=False,
    )
```

```python
import functools
import math

import jax
import jax.numpy as jnp
import numpy as np
from jax import lax
from jax.experimental import pallas as pl
from jax.experimental.pallas import tpu as pltpu
from jax.sharding import PartitionSpec as P

MESH = pl.DeviceIdType.MESH
ALPHA = 0.1
HALF_ROOT = math.sqrt(3.0) / 2.0
SWEEPS = 4
G = 8
T = 64
L = 128
Q = 4
C = 3
WIDE = Q * C * L
BLOCK = C * L
LO, MID, HI = 0, 5, 15
EXT = 18
FORTH = ((1, 2), (0, 1), (3, 1))
BACK = ((0, 1), (1, 1), (2, 2))
UNROLL = True
FAR = ((2, 1), (1, 1), (3, 1), (2, 0), (1, 0), (3, 0), (0, 1))


def tables():
    n = np.arange(T)
    forward = np.zeros((T, T))
    inverse = np.zeros((T, T))
    lam = np.zeros((2, T))
    beta = math.exp(math.log(ALPHA) / T)
    grow = ALPHA ** (n / T)
    for d in range(G):
        for half in range(2):
            for j in range(4):
                slot = 4 * d + j
                row = d * 8 + half * 4 + j
                if slot == 0:
                    freq, weight, part = 32 * half, 1.0, 0
                else:
                    freq, weight, part = slot, 2.0, half
                angle = 2.0 * math.pi * (freq * n % T) / T
                wave = np.cos(angle) if part == 0 else -np.sin(angle)
                forward[row] = wave * grow
                inverse[:, row] = weight * wave / grow / T
                lam[0, row] = 1.0 - beta * math.cos(2.0 * math.pi * freq / T)
                lam[1, row] = 0.0 if slot == 0 else beta * math.sin(2.0 * math.pi * freq / T)
    later = np.concatenate([forward[:, 8::8], np.zeros((T, 1))], axis=1)
    forward = np.concatenate([forward, later], axis=1)
    lam = np.broadcast_to(lam[:, :, None], (2, T, L))
    return [np.asarray(a, np.float32) for a in (forward, inverse, lam)]


def lanes(q, c):
    return pl.ds((q * C + c) * L, L)


def shift(tiles, step):
    lane = lax.broadcasted_iota(jnp.int32, (8, L), 1)
    turned = [pltpu.roll(t, step % L, axis=1) for t in tiles]
    edge = 0 if step == 1 else L - 1
    return [jnp.where(lane == edge, turned[(q - step) % Q], turned[q]) for q in range(Q)]


def permuted(tiles, order):
    out = []
    for q in range(Q):
        high = order[q] // L
        low = order[q] - high * L
        total = None
        for s in range(Q):
            part = jnp.take_along_axis(tiles[s], low, axis=1, mode="promise_in_bounds")
            total = part if total is None else jnp.where(high == s, part, total)
        out.append(total)
    return out


def couple(row, mid, low, up):
    s = HALF_ROOT
    h, u, v = range(3)
    diff = [[up[c][q] - low[c][q] for q in range(Q)] for c in range(3)]
    east = shift([mid[u][q] + 0.5 * low[u][q] - s * low[v][q] for q in range(Q)], -1)
    west = shift([mid[u][q] + 0.5 * up[u][q] - s * up[v][q] for q in range(Q)], 1)
    off_h = [east[q] - west[q] + 0.5 * diff[u][q] + s * diff[v][q] for q in range(Q)]
    low_m, up_p = shift(low[h], -1), shift(up[h], 1)
    mid_m, mid_p = shift(mid[h], -1), shift(mid[h], 1)
    off_u = [mid_m[q] - mid_p[q] + 0.5 * (diff[h][q] - up_p[q] + low_m[q]) for q in range(Q)]
    off_v = [s * (diff[h][q] + up_p[q] - low_m[q]) for q in range(Q)]
    return off_h, off_u, off_v


def load(ref, row):
    return [[ref[row, :, lanes(q, c)] for q in range(Q)] for c in range(C)]


def store(ref, row, tiles):
    for c in range(C):
        for q in range(Q):
            ref[row, :, lanes(q, c)] = tiles[c][q]


def wide(ref, q, i, row):
    return jnp.broadcast_to(ref[q, i, pl.ds(row, 1), :], (8, L))


def kernel(
    bands,
    it_any, fo_any, st_any, damp_any, cori_any, coup_any, order_any, fwd_any, inv_any, lam_any,
    out_ref,
    fwd_ref, inv_ref, lam_ref, it_v, fo_v, out_v, st_v, fixed,
    own_c, own_o, low_c, low_o, high_c, high_o, first,
    rows_t, halo_lo, halo_hi, coef, spec, cur,
    e_recv, a_send, a_recv, b_send, b_recv, c_send, c_recv, d_send, d_recv,
    in_sem, side_send, side_recv, e_ss, e_rs, a_ss, a_rs, b_ss, b_rs, c_ss, c_rs, d_ss, d_rs,
):
    me = lax.axis_index("tm")
    me_x, me_y = me // 2, lax.rem(me, 2)
    band = lax.axis_index("mesh")
    below = lax.rem(band + bands - 1, bands)
    above = lax.rem(band + 1, bands)
    peers = [lax.rem(me_x + dx, 4) * 2 + lax.rem(me_y + dy, 2) for dx, dy in FAR]

    barrier = pltpu.get_barrier_semaphore()
    for p in (below, above):
        pl.semaphore_signal(barrier, 1, device_id={"mesh": p}, device_id_type=MESH)
    for peer in peers:
        pl.semaphore_signal(barrier, 1, device_id={"tm": peer}, device_id_type=MESH)

    def by_lanes(wide_ref, tiled_ref, base):
        return [
            pltpu.make_async_copy(
                wide_ref.at[:, :, pl.ds(q * L, L)], tiled_ref.at[q, :, pl.ds(0, T), :], in_sem.at[base + q]
            )
            for q in range(Q)
        ]

    fields = by_lanes(it_any, it_v, 0)
    forces = by_lanes(fo_any, fo_v, 4)
    loads = [
        pltpu.make_async_copy(source, target, in_sem.at[8 + i])
        for i, (source, target) in enumerate(
            [
                (st_any, st_v), (damp_any, fixed.at[0]), (cori_any, fixed.at[1]), (coup_any, fixed.at[2]),
                (order_any, own_o), (fwd_any, fwd_ref), (inv_any, inv_ref), (lam_any, lam_ref),
            ]
        )
    ]

    for one in fields + forces + loads:
        one.start()
    sent = []

    def remote(src, dst, ss, rs, device):
        one = pltpu.make_async_remote_copy(
            src_ref=src, dst_ref=dst, send_sem=ss, recv_sem=rs, device_id=device, device_id_type=MESH
        )
        sent.append(one)
        return one

    def side(index, src, dst, p):
        return remote(src, dst, side_send.at[index], side_recv.at[index], {"mesh": p})

    class Hop:
        def __init__(self, src, dst, ss, rs, groups, index):
            part, base = pl.ds(*groups[index]), index * G

            def copy(peer):
                return pltpu.make_async_remote_copy(
                    src_ref=src.at[peer, part], dst_ref=dst.at[me, part],
                    send_sem=ss.at[base + peer], recv_sem=rs.at[base + peer],
                    device_id={"tm": peer}, device_id_type=MESH,
                )

            def out(peer):
                return pltpu.make_async_remote_copy(
                    src_ref=src.at[peer, part], dst_ref=dst.at[me, part],
                    send_sem=ss.at[base + peer], recv_sem=rs.at[base + me],
                    device_id={"tm": peer}, device_id_type=MESH,
                )

            self.copy, self.out = copy, out

        def half(self, half, act):
            for dx in (2, 1, 3):
                act(lax.rem(me_x + dx, 4) * 2 + half)
            pl.when(me_y != half)(lambda: act(me_x * 2 + half))

        def start(self):
            for peer in peers:
                self.out(peer).start()

        def arrive(self):
            for peer in peers:
                self.copy(peer).wait_recv()

        def start_half(self, half):
            self.half(half, lambda peer: self.out(peer).start())

        def arrive_half(self, half):
            self.half(half, lambda peer: self.copy(peer).wait_recv())

        def sent(self):
            for peer in peers:
                self.copy(peer).wait_send()

    def hops(src, dst, ss, rs, groups):
        return [Hop(src, dst, ss, rs, groups, i) for i in range(len(groups))]

    def start(copies):
        for one in copies:
            one.start()

    def arrive(copies):
        for one in copies:
            one.wait_recv()

    def keep(src, dst, group):
        for m in range(group[0], group[0] + group[1]):
            dst[me, m] = src[me, m]

    for one in fields:
        one.wait()
    for r in range(8):
        for c in range(C):
            for q in range(Q):
                rows_t[r + 1, :, lanes(q, c)] = it_v[q, c, pl.ds(r, 8, stride=8), :]
    for one in loads + forces:
        one.wait()
    for q in range(Q):
        for i in range(3):
            own_c[q, i] = fixed[i, :, pl.ds(q * L, L)]
            first[q, i] = jnp.where(me == 0, st_v[i, :, pl.ds(q * L, L)], 0.0)

    sub = lax.broadcasted_iota(jnp.int32, (8, L), 0)

    def residual_row(r, half, m):
        mid = load(rows_t, r + 1)
        off = couple(r, mid, load(rows_t, r), load(rows_t, r + 2))
        for q in range(Q):
            damp, cori, coup = [wide(own_c, q, i, r) for i in range(3)]
            h, u, v = mid[0][q], mid[1][q], mid[2][q]
            applied = [damp * h, damp * u - cori * v, damp * v + cori * u]
            for c in range(C):
                before = jnp.where(sub == 0, wide(first, q, c, r), pltpu.roll(mid[c][q], 1, axis=0))
                force = fo_v[q, c, pl.ds(r, 8, stride=8), :]
                a_send[2 * q + half, m, :, pl.ds(c * L, L)] = (
                    force + before - mid[c][q] - (applied[c] + coup * off[c][q])
                )

    def residual_pair(m, _):
        residual_row(3 - m, 0, m)
        residual_row(4 + m, 1, m)
        return 0

    lax.fori_loop(1, 3, residual_pair, 0, unroll=UNROLL)
    residual_pair(0, 0)

    pl.semaphore_wait(barrier, 9)
    halos = [side(0, rows_t.at[1], halo_hi, below), side(1, rows_t.at[8], halo_lo, above)]
    start(halos)
    last = pl.ds(T - 8, 8)
    hop_a = hops(a_send, a_recv, a_ss, a_rs, FORTH)
    hop_a[0].start()
    hop_e = [
        remote(it_v.at[peer // 2, :, last, :], e_recv.at[me], e_ss.at[k], e_rs.at[k], {"tm": peer})
        for k, peer in enumerate(peers)
    ]
    start(hop_e)
    hop_a[1].start()
    params = [
        side(2, own_c, high_c, below), side(3, own_c, low_c, above),
        side(4, own_o, high_o, below), side(5, own_o, low_o, above),
    ]
    start(params)
    e_recv[me] = it_v[me_x, :, last, :]
    keep(a_send, a_recv, FORTH[0])
    keep(a_send, a_recv, FORTH[1])

    def order(ref, which):
        return [jnp.broadcast_to(ref[pl.ds(which, 1), pl.ds(q * L, L)], (8, L)) for q in range(Q)]

    def halo(ref, row, which):
        tiles = [[ref[:, lanes(q, c)] for q in range(Q)] for c in range(C)]
        store(rows_t, row, [permuted(tiles[c], order(own_o, which)) for c in range(C)])

    arrive(halos[:1])
    halo(halo_hi, 9, 1)
    residual_row(7, 1, 3)
    hop_a[2].start_half(1)
    arrive(halos[1:])
    halo(halo_lo, 0, 0)
    residual_row(0, 0, 3)
    hop_a[2].start_half(0)
    keep(a_send, a_recv, FORTH[2])

    lam_re = lam_ref[0, pl.ds(me * 8, 8), :]
    lam_im = lam_ref[1, pl.ds(me * 8, 8), :]
    sign = jnp.where(sub < 4, -1.0, 1.0)

    def coef_row(ref, offset):
        def body(r, _):
            for q in range(Q):
                damp, cori, coup = [wide(ref, q, i, r) for i in range(3)]
                a_re = lam_re + damp
                a_im = lam_im
                inv = 1.0 / (a_re * a_re + a_im * a_im)
                d_re = a_re * a_re - a_im * a_im + cori * cori
                d_im = 2.0 * a_re * a_im
                d_inv = 1.0 / (d_re * d_re + d_im * d_im)
                seven = [
                    a_re * inv,
                    -sign * a_im * inv,
                    (a_re * d_re + a_im * d_im) * d_inv,
                    sign * (a_im * d_re - a_re * d_im) * d_inv,
                    cori * d_re * d_inv,
                    -sign * cori * d_im * d_inv,
                    coup,
                ]
                for i in range(7):
                    coef[r + offset, i, :, pl.ds(q * L, L)] = seven[i]
            return 0

        return body

    lax.fori_loop(0, 8, coef_row(own_c, MID), 0)

    def transform(table, src, dst, m, extra):
        rows = src[:, m].reshape(T, BLOCK)
        if extra is not None:
            rows = jnp.concatenate([rows, extra], axis=0)
        dst[:, m] = jnp.dot(
            table, rows, precision=lax.Precision.HIGHEST, preferred_element_type=jnp.float32
        ).reshape(G, 8, BLOCK)

    def previous(m):
        row = 3 - m + me_y * (1 + 2 * m)
        return jnp.concatenate([e_flat(c, row) for c in range(C)], axis=1)

    def e_flat(c, row):
        return e_recv.reshape((G + 1) * C * 8, L)[pl.ds(c * 8 + row, G, stride=C * 8), :]

    arrive(hop_e)
    hop_b = hops(b_send, b_recv, b_ss, b_rs, FORTH)
    for i, (begin, count) in enumerate(FORTH):
        hop_a[i].arrive()
        for m in range(begin, begin + count):
            transform(fwd_ref[...], a_recv, b_send, m, previous(m))
        hop_b[i].start()
        keep(b_send, b_recv, FORTH[i])

    arrive(params)
    lax.fori_loop(5, 8, coef_row(low_c, LO - 5), 0)
    lax.fori_loop(0, 3, coef_row(high_c, HI), 0)

    def solve(row, x):
        out = [[], [], []]
        for q in range(Q):
            k = [coef[row, i, :, pl.ds(q * L, L)] for i in range(6)]
            xh, xu, xv = x[0][q], x[1][q], x[2][q]
            sh, su, sv = [pltpu.roll(t, 4, axis=0) for t in (xh, xu, xv)]
            out[0].append(k[0] * xh + k[1] * sh)
            out[1].append(k[2] * xu + k[3] * su + (k[4] * xv + k[5] * sv))
            out[2].append(k[2] * xv + k[3] * sv - (k[4] * xu + k[5] * su))
        return out

    def first_row(row):
        store(cur.at[0], row, solve(row, load(spec, row)))

    def sweep_row(level, row):
        src = cur.at[level]
        off = couple(row, load(src, row), load(src, row - 1), load(src, row + 1))
        full = load(spec, row)
        x = [
            [full[c][q] - coef[row, 6, :, pl.ds(q * L, L)] * off[c][q] for q in range(Q)]
            for c in range(C)
        ]
        return solve(row, x)

    def sweep_pair(level, low, high):
        def body(i, _):
            store(cur.at[level + 1], low + i, sweep_row(level, low + i))
            store(cur.at[level + 1], high - i, sweep_row(level, high - i))
            return 0

        return body

    def ghost(level, to, source, ref, which):
        src = cur.at[level]
        tiles = load(src, source)
        store(src, to, [permuted(tiles[c], order(ref, which)) for c in range(C)])

    def own_row(half, m):
        r = 4 + m if half else 3 - m
        for q in range(Q):
            for c in range(C):
                spec[MID + r, :, lanes(q, c)] = b_recv[2 * q + half, m, :, pl.ds(c * L, L)]

    def own_rows(m, _):
        own_row(0, m)
        own_row(1, m)
        return 0

    def own_first(m, _):
        first_row(MID + 3 - m)
        first_row(MID + 4 + m)
        return 0

    def rim(index, src, dst, count, p):
        return side(index, spec.at[pl.ds(src, count)], spec.at[pl.ds(dst, count)], p)

    rims = [
        rim(6, MID + 1, HI + 1, 2, below), rim(7, MID, HI, 1, below),
        rim(8, MID + 5, LO, 2, above), rim(9, MID + 7, LO + 2, 1, above),
    ]
    hop_b[0].arrive()
    lax.fori_loop(1, 3, own_rows, 0, unroll=UNROLL)
    start([rims[0], rims[2]])
    lax.fori_loop(1, 3, own_first, 0, unroll=UNROLL)
    hop_b[1].arrive()
    own_rows(0, 0)
    own_first(0, 0)
    lax.fori_loop(0, 2, sweep_pair(0, MID + 2, MID + 5), 0, unroll=UNROLL)
    hop_b[2].arrive_half(1)
    own_row(1, 3)
    start(rims[3:])
    hop_b[2].arrive_half(0)
    own_row(0, 3)
    start(rims[1:2])
    own_first(3, 0)
    ghost(0, LO + 3, MID, low_o, 1)
    ghost(0, HI - 1, MID + 7, high_o, 0)
    lax.fori_loop(0, 1, sweep_pair(0, MID + 1, MID + 6), 0)
    lax.fori_loop(0, 2, sweep_pair(1, MID + 2, MID + 5), 0, unroll=UNROLL)

    hop_c = hops(c_send, c_recv, c_ss, c_rs, BACK)

    def last_row(half, m):
        tiles = sweep_row(2, MID + (4 + m if half else 3 - m))
        for q in range(Q):
            for c in range(C):
                c_send[2 * q + half, m, :, pl.ds(c * L, L)] = tiles[c][q]

    def sweep_rows(level, first_one):
        def body(i, _):
            store(cur.at[level + 1], first_one + i, sweep_row(level, first_one + i))
            return 0

        lax.fori_loop(0, 2, body, 0, unroll=UNROLL)

    def rim_first(first_one):
        def body(i, _):
            first_row(first_one + i)
            return 0

        lax.fori_loop(0, 3, body, 0, unroll=UNROLL)

    def finish(half, i):
        begin, count = BACK[i]

        def body(m, _):
            last_row(half, m)
            return 0

        lax.fori_loop(begin, begin + count, body, 0, unroll=UNROLL)
        hop_c[i].start_half(half)

    last_row(0, 0)
    last_row(1, 0)
    hop_c[0].start()
    arrive(rims[:2])
    rim_first(HI)
    ghost(0, MID + 8, HI, own_o, 1)
    sweep_rows(0, HI)
    store(cur.at[1], MID + 7, sweep_row(0, MID + 7))
    ghost(1, HI - 1, MID + 7, high_o, 0)
    ghost(1, MID + 8, HI, own_o, 1)
    store(cur.at[2], HI, sweep_row(1, HI))
    sweep_rows(1, MID + 6)
    finish(1, 1)
    ghost(2, MID + 8, HI, own_o, 1)
    finish(1, 2)
    arrive(rims[2:3])
    first_row(LO)
    first_row(LO + 1)
    arrive(rims[3:])
    first_row(LO + 2)
    ghost(0, MID - 1, LO + 2, own_o, 0)
    sweep_rows(0, LO + 1)
    store(cur.at[1], MID, sweep_row(0, MID))
    ghost(1, LO + 3, MID, low_o, 1)
    ghost(1, MID - 1, LO + 2, own_o, 0)
    store(cur.at[2], LO + 2, sweep_row(1, LO + 2))
    sweep_rows(1, MID)
    finish(0, 1)
    ghost(2, MID - 1, LO + 2, own_o, 0)
    finish(0, 2)
    for group in BACK:
        keep(c_send, c_recv, group)

    for one in sent:
        one.wait_send()
    for one in hop_a + hop_b:
        one.sent()
    hop_d = hops(d_send, d_recv, d_ss, d_rs, BACK)
    for i, (begin, count) in enumerate(BACK):
        hop_c[i].arrive()
        for m in range(begin, begin + count):
            transform(inv_ref[...], c_recv, d_send, m, None)
        hop_d[i].start()
        keep(d_send, d_recv, BACK[i])
    for one in hop_c:
        one.sent()
    for half in (1, 0):
        for i, (begin, count) in enumerate(BACK):
            hop_d[i].arrive_half(half)
            for m in range(begin, begin + count):
                r = 4 + m if half else 3 - m
                for q in range(Q):
                    for c in range(C):
                        out_v[q, c, pl.ds(r, 8, stride=8), :] = (
                            rows_t[r + 1, :, lanes(q, c)] + d_recv[2 * q + half, m, :, pl.ds(c * L, L)]
                        )
    for q in range(Q):
        for c in range(C):
            out_ref[c, :, pl.ds(q * L, L)] = out_v[q, c, pl.ds(0, T), :]
    for one in hop_d:
        one.sent()


def on_device(bands, iterate, forcing, start_state, damping, coriolis, coupling, edge_order):
    forward, inverse, lam = tables()
    flat = (C, T, Q * L)
    hbm = pl.BlockSpec(memory_space=pltpu.HBM)
    f32, i32 = jnp.float32, jnp.int32
    block = pltpu.VMEM((G, 4, 8, BLOCK), f32)
    staged = pltpu.VMEM((3, 8, Q * L), f32)
    own, pair = pltpu.VMEM((Q, 3, 8, L), f32), pltpu.VMEM((2, Q * L), i32)
    tiled = pltpu.VMEM((Q, C, T + 8, L), f32)
    row = pltpu.VMEM((8, WIDE), f32)
    dma = pltpu.SemaphoreType.DMA
    out = pl.pallas_call(
        functools.partial(kernel, bands),
        out_shape=pltpu.VMEM(flat, f32),
        in_specs=[hbm] * 10,
        out_specs=pl.BlockSpec(memory_space=pltpu.VMEM),
        scratch_shapes=[
            pltpu.VMEM((T, T + 8), f32), pltpu.VMEM((T, T), f32), pltpu.VMEM((2, T, L), f32),
            tiled, tiled, tiled, staged, staged,
            own, pair, own, pair, own, pair, own,
            pltpu.VMEM((10, 8, WIDE), f32), row, row,
            pltpu.VMEM((EXT, 7, 8, Q * L), f32),
            pltpu.VMEM((EXT, 8, WIDE), f32),
            pltpu.VMEM((SWEEPS, EXT, 8, WIDE), f32),
            pltpu.VMEM((G + 1, C, 8, L), f32),
        ]
        + [block] * 8
        + [dma((16,)), dma((10,)), dma((10,)), dma((7,)), dma((7,))]
        + [dma((G * len(FORTH),))] * 4
        + [dma((G * len(BACK),))] * 4,
        compiler_params=pltpu.CompilerParams(
            collective_id=0, has_side_effects=True, vmem_limit_bytes=40 * 1024 * 1024
        ),
    )(
        *[
            pltpu.with_memory_space_constraint(jnp.asarray(x), pltpu.HBM)
            for x in (
                iterate.reshape(flat), forcing.reshape(flat), start_state, damping, coriolis, coupling,
                edge_order.reshape(2, Q * L), forward, inverse, lam,
            )
        ]
    )
    return out.reshape(iterate.shape)


def solution(mesh):
    in_specs = (
        P(None, "tm", "mesh", None),
        P(None, "tm", "mesh", None),
        P(None, "mesh", None),
        P("mesh", None),
        P("mesh", None),
        P("mesh", None),
        P("mesh", None, None),
    )
    return jax.shard_map(
        functools.partial(on_device, mesh.shape["mesh"]),
        mesh=mesh, in_specs=in_specs, out_specs=P(None, "tm", "mesh", None), check_vma=False,
    )
```

```python
import functools
import math

import jax
import jax.numpy as jnp
import numpy as np
from jax import lax
from jax.experimental import pallas as pl
from jax.experimental.pallas import tpu as pltpu
from jax.sharding import PartitionSpec as P

MESH = pl.DeviceIdType.MESH
ALPHA = 0.1
HALF_ROOT = math.sqrt(3.0) / 2.0
SWEEPS = 4
G = 8
T = 64
L = 128
Q = 4
C = 3
WIDE = Q * C * L
BLOCK = C * L
LO, MID, HI = 0, 5, 15
EXT = 18
FORTH = ((1, 2), (0, 1), (3, 1))
BACK = ((0, 1), (1, 1), (2, 2))
UNROLL = True
FAR = ((2, 1), (1, 1), (3, 1), (2, 0), (1, 0), (3, 0), (0, 1))


def split(table):
    parts, rest = [], np.asarray(table, np.float32)
    for _ in range(3):
        parts.append(rest.astype(jnp.bfloat16))
        rest = rest - parts[-1].astype(np.float32)
    one, two, three = parts
    return np.stack([np.concatenate([one, one, two], axis=1), np.concatenate([two, one, three], axis=1)])


def tables():
    n = np.arange(T)
    forward = np.zeros((T, T))
    inverse = np.zeros((T, T))
    lam = np.zeros((2, T))
    beta = math.exp(math.log(ALPHA) / T)
    grow = ALPHA ** (n / T)
    for d in range(G):
        for half in range(2):
            for j in range(4):
                slot = 4 * d + j
                row = d * 8 + half * 4 + j
                if slot == 0:
                    freq, weight, part = 32 * half, 1.0, 0
                else:
                    freq, weight, part = slot, 2.0, half
                angle = 2.0 * math.pi * (freq * n % T) / T
                wave = np.cos(angle) if part == 0 else -np.sin(angle)
                forward[row] = wave * grow
                inverse[:, row] = weight * wave / grow / T
                lam[0, row] = 1.0 - beta * math.cos(2.0 * math.pi * freq / T)
                lam[1, row] = 0.0 if slot == 0 else beta * math.sin(2.0 * math.pi * freq / T)
    later = np.concatenate([forward[:, 8::8], np.zeros((T, 9))], axis=1)
    forward = np.concatenate([forward, later], axis=1)
    lam = np.broadcast_to(lam[:, :, None], (2, T, L))
    return [split(forward), split(inverse), np.asarray(lam, np.float32)]


def lanes(q, c):
    return pl.ds((q * C + c) * L, L)


def shift(tiles, step):
    lane = lax.broadcasted_iota(jnp.int32, (8, L), 1)
    turned = [pltpu.roll(t, step % L, axis=1) for t in tiles]
    edge = 0 if step == 1 else L - 1
    return [jnp.where(lane == edge, turned[(q - step) % Q], turned[q]) for q in range(Q)]


def permuted(tiles, order):
    out = []
    for q in range(Q):
        high = order[q] // L
        low = order[q] - high * L
        total = None
        for s in range(Q):
            part = jnp.take_along_axis(tiles[s], low, axis=1, mode="promise_in_bounds")
            total = part if total is None else jnp.where(high == s, part, total)
        out.append(total)
    return out


def couple(row, mid, low, up):
    s = HALF_ROOT
    h, u, v = range(3)
    diff = [[up[c][q] - low[c][q] for q in range(Q)] for c in range(3)]
    east = shift([mid[u][q] + 0.5 * low[u][q] - s * low[v][q] for q in range(Q)], -1)
    west = shift([mid[u][q] + 0.5 * up[u][q] - s * up[v][q] for q in range(Q)], 1)
    off_h = [east[q] - west[q] + 0.5 * diff[u][q] + s * diff[v][q] for q in range(Q)]
    low_m, up_p = shift(low[h], -1), shift(up[h], 1)
    mid_m, mid_p = shift(mid[h], -1), shift(mid[h], 1)
    off_u = [mid_m[q] - mid_p[q] + 0.5 * (diff[h][q] - up_p[q] + low_m[q]) for q in range(Q)]
    off_v = [s * (diff[h][q] + up_p[q] - low_m[q]) for q in range(Q)]
    return off_h, off_u, off_v


def load(ref, row):
    return [[ref[row, :, lanes(q, c)] for q in range(Q)] for c in range(C)]


def store(ref, row, tiles):
    for c in range(C):
        for q in range(Q):
            ref[row, :, lanes(q, c)] = tiles[c][q]


def wide(ref, q, i, row):
    return jnp.broadcast_to(ref[q, i, pl.ds(row, 1), :], (8, L))


def kernel(
    bands,
    it_any, fo_any, st_any, damp_any, cori_any, coup_any, order_any, fwd_any, inv_any, lam_any,
    out_ref,
    fwd_ref, inv_ref, lam_ref, it_v, fo_v, out_v, st_v, fixed,
    own_c, own_o, low_c, low_o, high_c, high_o, first,
    rows_t, halo_lo, halo_hi, coef, spec, cur,
    e_recv, a_send, a_recv, b_send, b_recv, c_send, c_recv, d_send, d_recv,
    in_sem, side_send, side_recv, e_ss, e_rs, a_ss, a_rs, b_ss, b_rs, c_ss, c_rs, d_ss, d_rs,
):
    me = lax.axis_index("tm")
    me_x, me_y = me // 2, lax.rem(me, 2)
    band = lax.axis_index("mesh")
    below = lax.rem(band + bands - 1, bands)
    above = lax.rem(band + 1, bands)
    peers = [lax.rem(me_x + dx, 4) * 2 + lax.rem(me_y + dy, 2) for dx, dy in FAR]

    barrier = pltpu.get_barrier_semaphore()
    for p in (below, above):
        pl.semaphore_signal(barrier, 1, device_id={"mesh": p}, device_id_type=MESH)
    for peer in peers:
        pl.semaphore_signal(barrier, 1, device_id={"tm": peer}, device_id_type=MESH)

    def by_lanes(wide_ref, tiled_ref, base):
        return [
            pltpu.make_async_copy(
                wide_ref.at[:, :, pl.ds(q * L, L)], tiled_ref.at[q, :, pl.ds(0, T), :], in_sem.at[base + q]
            )
            for q in range(Q)
        ]

    fields = by_lanes(it_any, it_v, 0)
    forces = by_lanes(fo_any, fo_v, 4)
    loads = [
        pltpu.make_async_copy(source, target, in_sem.at[8 + i])
        for i, (source, target) in enumerate(
            [
                (st_any, st_v), (damp_any, fixed.at[0]), (cori_any, fixed.at[1]), (coup_any, fixed.at[2]),
                (order_any, own_o), (fwd_any, fwd_ref), (inv_any, inv_ref), (lam_any, lam_ref),
            ]
        )
    ]

    for one in fields + forces + loads:
        one.start()
    sent = []

    def remote(src, dst, ss, rs, device):
        one = pltpu.make_async_remote_copy(
            src_ref=src, dst_ref=dst, send_sem=ss, recv_sem=rs, device_id=device, device_id_type=MESH
        )
        sent.append(one)
        return one

    def side(index, src, dst, p):
        return remote(src, dst, side_send.at[index], side_recv.at[index], {"mesh": p})

    class Hop:
        def __init__(self, src, dst, ss, rs, groups, index):
            part, base = pl.ds(*groups[index]), index * G

            def copy(peer):
                return pltpu.make_async_remote_copy(
                    src_ref=src.at[peer, part], dst_ref=dst.at[me, part],
                    send_sem=ss.at[base + peer], recv_sem=rs.at[base + peer],
                    device_id={"tm": peer}, device_id_type=MESH,
                )

            def out(peer):
                return pltpu.make_async_remote_copy(
                    src_ref=src.at[peer, part], dst_ref=dst.at[me, part],
                    send_sem=ss.at[base + peer], recv_sem=rs.at[base + me],
                    device_id={"tm": peer}, device_id_type=MESH,
                )

            self.copy, self.out = copy, out

        def half(self, half, act):
            for dx in (2, 1, 3):
                act(lax.rem(me_x + dx, 4) * 2 + half)
            pl.when(me_y != half)(lambda: act(me_x * 2 + half))

        def start(self):
            for peer in peers:
                self.out(peer).start()

        def arrive(self):
            for peer in peers:
                self.copy(peer).wait_recv()

        def start_half(self, half):
            self.half(half, lambda peer: self.out(peer).start())

        def arrive_half(self, half):
            self.half(half, lambda peer: self.copy(peer).wait_recv())

        def sent(self):
            for peer in peers:
                self.copy(peer).wait_send()

    def hops(src, dst, ss, rs, groups):
        return [Hop(src, dst, ss, rs, groups, i) for i in range(len(groups))]

    def start(copies):
        for one in copies:
            one.start()

    def arrive(copies):
        for one in copies:
            one.wait_recv()

    def keep(src, dst, group):
        for m in range(group[0], group[0] + group[1]):
            dst[me, m] = src[me, m]

    for one in fields:
        one.wait()
    for r in range(8):
        for c in range(C):
            for q in range(Q):
                rows_t[r + 1, :, lanes(q, c)] = it_v[q, c, pl.ds(r, 8, stride=8), :]
    for one in loads + forces:
        one.wait()
    for q in range(Q):
        for i in range(3):
            own_c[q, i] = fixed[i, :, pl.ds(q * L, L)]
            first[q, i] = jnp.where(me == 0, st_v[i, :, pl.ds(q * L, L)], 0.0)

    sub = lax.broadcasted_iota(jnp.int32, (8, L), 0)

    def residual_row(r, half, m):
        mid = load(rows_t, r + 1)
        off = couple(r, mid, load(rows_t, r), load(rows_t, r + 2))
        for q in range(Q):
            damp, cori, coup = [wide(own_c, q, i, r) for i in range(3)]
            h, u, v = mid[0][q], mid[1][q], mid[2][q]
            applied = [damp * h, damp * u - cori * v, damp * v + cori * u]
            for c in range(C):
                before = jnp.where(sub == 0, wide(first, q, c, r), pltpu.roll(mid[c][q], 1, axis=0))
                force = fo_v[q, c, pl.ds(r, 8, stride=8), :]
                a_send[2 * q + half, m, :, pl.ds(c * L, L)] = (
                    force + before - mid[c][q] - (applied[c] + coup * off[c][q])
                )

    def residual_pair(m, _):
        residual_row(3 - m, 0, m)
        residual_row(4 + m, 1, m)
        return 0

    lax.fori_loop(1, 3, residual_pair, 0, unroll=UNROLL)
    residual_pair(0, 0)

    pl.semaphore_wait(barrier, 9)
    halos = [side(0, rows_t.at[1], halo_hi, below), side(1, rows_t.at[8], halo_lo, above)]
    start(halos)
    last = pl.ds(T - 8, 8)
    hop_a = hops(a_send, a_recv, a_ss, a_rs, FORTH)
    hop_a[0].start()
    hop_e = [
        remote(it_v.at[peer // 2, :, last, :], e_recv.at[me], e_ss.at[k], e_rs.at[k], {"tm": peer})
        for k, peer in enumerate(peers)
    ]
    start(hop_e)
    hop_a[1].start()
    params = [
        side(2, own_c, high_c, below), side(3, own_c, low_c, above),
        side(4, own_o, high_o, below), side(5, own_o, low_o, above),
    ]
    start(params)
    e_recv[me] = it_v[me_x, :, last, :]
    keep(a_send, a_recv, FORTH[0])
    keep(a_send, a_recv, FORTH[1])

    def order(ref, which):
        return [jnp.broadcast_to(ref[pl.ds(which, 1), pl.ds(q * L, L)], (8, L)) for q in range(Q)]

    def halo(ref, row, which):
        tiles = [[ref[:, lanes(q, c)] for q in range(Q)] for c in range(C)]
        store(rows_t, row, [permuted(tiles[c], order(own_o, which)) for c in range(C)])

    arrive(halos[:1])
    halo(halo_hi, 9, 1)
    residual_row(7, 1, 3)
    hop_a[2].start_half(1)
    arrive(halos[1:])
    halo(halo_lo, 0, 0)
    residual_row(0, 0, 3)
    hop_a[2].start_half(0)
    keep(a_send, a_recv, FORTH[2])

    lam_re = lam_ref[0, pl.ds(me * 8, 8), :]
    lam_im = lam_ref[1, pl.ds(me * 8, 8), :]
    sign = jnp.where(sub < 4, -1.0, 1.0)

    def coef_row(ref, offset):
        def body(r, _):
            for q in range(Q):
                damp, cori, coup = [wide(ref, q, i, r) for i in range(3)]
                a_re = lam_re + damp
                a_im = lam_im
                inv = 1.0 / (a_re * a_re + a_im * a_im)
                d_re = a_re * a_re - a_im * a_im + cori * cori
                d_im = 2.0 * a_re * a_im
                d_inv = 1.0 / (d_re * d_re + d_im * d_im)
                seven = [
                    a_re * inv,
                    -sign * a_im * inv,
                    (a_re * d_re + a_im * d_im) * d_inv,
                    sign * (a_im * d_re - a_re * d_im) * d_inv,
                    cori * d_re * d_inv,
                    -sign * cori * d_im * d_inv,
                    coup,
                ]
                for i in range(7):
                    coef[r + offset, i, :, pl.ds(q * L, L)] = seven[i]
            return 0

        return body

    lax.fori_loop(0, 8, coef_row(own_c, MID), 0)

    def transform(table, src, dst, m, extra):
        rows = src[:, m].reshape(T, BLOCK)
        if extra is not None:
            rows = jnp.concatenate([rows, extra, jnp.zeros((8, BLOCK), jnp.float32)], axis=0)
        parts = []
        for _ in range(3):
            parts.append(rows.astype(jnp.bfloat16))
            rows = rows - parts[-1].astype(jnp.float32)
        one, two, three = parts
        small = jnp.dot(
            table[1], jnp.concatenate([two, three, one], axis=0), preferred_element_type=jnp.float32
        )
        large = jnp.dot(
            table[0], jnp.concatenate([one, two, one], axis=0), preferred_element_type=jnp.float32
        )
        dst[:, m] = (large + small).reshape(G, 8, BLOCK)

    def previous(m):
        row = 3 - m + me_y * (1 + 2 * m)
        return jnp.concatenate([e_flat(c, row) for c in range(C)], axis=1)

    def e_flat(c, row):
        return e_recv.reshape((G + 1) * C * 8, L)[pl.ds(c * 8 + row, G, stride=C * 8), :]

    arrive(hop_e)
    hop_b = hops(b_send, b_recv, b_ss, b_rs, FORTH)
    for i, (begin, count) in enumerate(FORTH):
        hop_a[i].arrive()
        for m in range(begin, begin + count):
            transform(fwd_ref, a_recv, b_send, m, previous(m))
        hop_b[i].start()
        keep(b_send, b_recv, FORTH[i])

    arrive(params)
    lax.fori_loop(5, 8, coef_row(low_c, LO - 5), 0)
    lax.fori_loop(0, 3, coef_row(high_c, HI), 0)

    def solve(row, x):
        out = [[], [], []]
        for q in range(Q):
            k = [coef[row, i, :, pl.ds(q * L, L)] for i in range(6)]
            xh, xu, xv = x[0][q], x[1][q], x[2][q]
            sh, su, sv = [pltpu.roll(t, 4, axis=0) for t in (xh, xu, xv)]
            out[0].append(k[0] * xh + k[1] * sh)
            out[1].append(k[2] * xu + k[3] * su + (k[4] * xv + k[5] * sv))
            out[2].append(k[2] * xv + k[3] * sv - (k[4] * xu + k[5] * su))
        return out

    def first_row(row):
        store(cur.at[0], row, solve(row, load(spec, row)))

    def sweep_row(level, row):
        src = cur.at[level]
        off = couple(row, load(src, row), load(src, row - 1), load(src, row + 1))
        full = load(spec, row)
        x = [
            [full[c][q] - coef[row, 6, :, pl.ds(q * L, L)] * off[c][q] for q in range(Q)]
            for c in range(C)
        ]
        return solve(row, x)

    def sweep_pair(level, low, high):
        def body(i, _):
            store(cur.at[level + 1], low + i, sweep_row(level, low + i))
            store(cur.at[level + 1], high - i, sweep_row(level, high - i))
            return 0

        return body

    def ghost(level, to, source, ref, which):
        src = cur.at[level]
        tiles = load(src, source)
        store(src, to, [permuted(tiles[c], order(ref, which)) for c in range(C)])

    def own_row(half, m):
        r = 4 + m if half else 3 - m
        for q in range(Q):
            for c in range(C):
                spec[MID + r, :, lanes(q, c)] = b_recv[2 * q + half, m, :, pl.ds(c * L, L)]

    def own_rows(m, _):
        own_row(0, m)
        own_row(1, m)
        return 0

    def own_first(m, _):
        first_row(MID + 3 - m)
        first_row(MID + 4 + m)
        return 0

    def rim(index, src, dst, count, p):
        return side(index, spec.at[pl.ds(src, count)], spec.at[pl.ds(dst, count)], p)

    rims = [
        rim(6, MID + 1, HI + 1, 2, below), rim(7, MID, HI, 1, below),
        rim(8, MID + 5, LO, 2, above), rim(9, MID + 7, LO + 2, 1, above),
    ]
    hop_b[0].arrive()
    lax.fori_loop(1, 3, own_rows, 0, unroll=UNROLL)
    start([rims[0], rims[2]])
    lax.fori_loop(1, 3, own_first, 0, unroll=UNROLL)
    hop_b[1].arrive()
    own_rows(0, 0)
    own_first(0, 0)
    lax.fori_loop(0, 2, sweep_pair(0, MID + 2, MID + 5), 0, unroll=UNROLL)
    hop_b[2].arrive_half(1)
    own_row(1, 3)
    start(rims[3:])
    hop_b[2].arrive_half(0)
    own_row(0, 3)
    start(rims[1:2])
    own_first(3, 0)
    ghost(0, LO + 3, MID, low_o, 1)
    ghost(0, HI - 1, MID + 7, high_o, 0)
    lax.fori_loop(0, 1, sweep_pair(0, MID + 1, MID + 6), 0)
    lax.fori_loop(0, 2, sweep_pair(1, MID + 2, MID + 5), 0, unroll=UNROLL)

    hop_c = hops(c_send, c_recv, c_ss, c_rs, BACK)

    def last_row(half, m):
        tiles = sweep_row(2, MID + (4 + m if half else 3 - m))
        for q in range(Q):
            for c in range(C):
                c_send[2 * q + half, m, :, pl.ds(c * L, L)] = tiles[c][q]

    def sweep_rows(level, first_one):
        def body(i, _):
            store(cur.at[level + 1], first_one + i, sweep_row(level, first_one + i))
            return 0

        lax.fori_loop(0, 2, body, 0, unroll=UNROLL)

    def rim_first(first_one):
        def body(i, _):
            first_row(first_one + i)
            return 0

        lax.fori_loop(0, 3, body, 0, unroll=UNROLL)

    def finish(half, i):
        begin, count = BACK[i]

        def body(m, _):
            last_row(half, m)
            return 0

        lax.fori_loop(begin, begin + count, body, 0, unroll=UNROLL)
        hop_c[i].start_half(half)

    last_row(0, 0)
    last_row(1, 0)
    hop_c[0].start()
    arrive(rims[:2])
    rim_first(HI)
    ghost(0, MID + 8, HI, own_o, 1)
    sweep_rows(0, HI)
    store(cur.at[1], MID + 7, sweep_row(0, MID + 7))
    ghost(1, HI - 1, MID + 7, high_o, 0)
    ghost(1, MID + 8, HI, own_o, 1)
    store(cur.at[2], HI, sweep_row(1, HI))
    sweep_rows(1, MID + 6)
    finish(1, 1)
    ghost(2, MID + 8, HI, own_o, 1)
    finish(1, 2)
    arrive(rims[2:3])
    first_row(LO)
    first_row(LO + 1)
    arrive(rims[3:])
    first_row(LO + 2)
    ghost(0, MID - 1, LO + 2, own_o, 0)
    sweep_rows(0, LO + 1)
    store(cur.at[1], MID, sweep_row(0, MID))
    ghost(1, LO + 3, MID, low_o, 1)
    ghost(1, MID - 1, LO + 2, own_o, 0)
    store(cur.at[2], LO + 2, sweep_row(1, LO + 2))
    sweep_rows(1, MID)
    finish(0, 1)
    ghost(2, MID - 1, LO + 2, own_o, 0)
    finish(0, 2)
    for group in BACK:
        keep(c_send, c_recv, group)

    for one in sent:
        one.wait_send()
    for one in hop_a + hop_b:
        one.sent()
    hop_d = hops(d_send, d_recv, d_ss, d_rs, BACK)
    for i, (begin, count) in enumerate(BACK):
        hop_c[i].arrive()
        for m in range(begin, begin + count):
            transform(inv_ref, c_recv, d_send, m, None)
        hop_d[i].start()
        keep(d_send, d_recv, BACK[i])
    for one in hop_c:
        one.sent()
    for half in (1, 0):
        for i, (begin, count) in enumerate(BACK):
            hop_d[i].arrive_half(half)
            for m in range(begin, begin + count):
                r = 4 + m if half else 3 - m
                for q in range(Q):
                    for c in range(C):
                        out_v[q, c, pl.ds(r, 8, stride=8), :] = (
                            rows_t[r + 1, :, lanes(q, c)] + d_recv[2 * q + half, m, :, pl.ds(c * L, L)]
                        )
    for q in range(Q):
        for c in range(C):
            out_ref[c, :, pl.ds(q * L, L)] = out_v[q, c, pl.ds(0, T), :]
    for one in hop_d:
        one.sent()


def on_device(bands, iterate, forcing, start_state, damping, coriolis, coupling, edge_order):
    forward, inverse, lam = tables()
    flat = (C, T, Q * L)
    hbm = pl.BlockSpec(memory_space=pltpu.HBM)
    f32, i32 = jnp.float32, jnp.int32
    block = pltpu.VMEM((G, 4, 8, BLOCK), f32)
    staged = pltpu.VMEM((3, 8, Q * L), f32)
    own, pair = pltpu.VMEM((Q, 3, 8, L), f32), pltpu.VMEM((2, Q * L), i32)
    tiled = pltpu.VMEM((Q, C, T + 8, L), f32)
    row = pltpu.VMEM((8, WIDE), f32)
    dma = pltpu.SemaphoreType.DMA
    out = pl.pallas_call(
        functools.partial(kernel, bands),
        out_shape=pltpu.VMEM(flat, f32),
        in_specs=[hbm] * 10,
        out_specs=pl.BlockSpec(memory_space=pltpu.VMEM),
        scratch_shapes=[
            pltpu.VMEM((2, T, 3 * (T + 16)), jnp.bfloat16), pltpu.VMEM((2, T, 3 * T), jnp.bfloat16), pltpu.VMEM((2, T, L), f32),
            tiled, tiled, tiled, staged, staged,
            own, pair, own, pair, own, pair, own,
            pltpu.VMEM((10, 8, WIDE), f32), row, row,
            pltpu.VMEM((EXT, 7, 8, Q * L), f32),
            pltpu.VMEM((EXT, 8, WIDE), f32),
            pltpu.VMEM((SWEEPS, EXT, 8, WIDE), f32),
            pltpu.VMEM((G + 1, C, 8, L), f32),
        ]
        + [block] * 8
        + [dma((16,)), dma((10,)), dma((10,)), dma((7,)), dma((7,))]
        + [dma((G * len(FORTH),))] * 4
        + [dma((G * len(BACK),))] * 4,
        compiler_params=pltpu.CompilerParams(
            collective_id=0, has_side_effects=True, vmem_limit_bytes=40 * 1024 * 1024
        ),
    )(
        *[
            pltpu.with_memory_space_constraint(jnp.asarray(x), pltpu.HBM)
            for x in (
                iterate.reshape(flat), forcing.reshape(flat), start_state, damping, coriolis, coupling,
                edge_order.reshape(2, Q * L), forward, inverse, lam,
            )
        ]
    )
    return out.reshape(iterate.shape)


def solution(mesh):
    in_specs = (
        P(None, "tm", "mesh", None),
        P(None, "tm", "mesh", None),
        P(None, "mesh", None),
        P("mesh", None),
        P("mesh", None),
        P("mesh", None),
        P("mesh", None, None),
    )
    return jax.shard_map(
        functools.partial(on_device, mesh.shape["mesh"]),
        mesh=mesh, in_specs=in_specs, out_specs=P(None, "tm", "mesh", None), check_vma=False,
    )
```
